512 devices in a mesh: seq: 64 (over y, z_lo, x), wt: 8 (over z_hi, core).
Axes of the slice: x: 4, y: 8, z: 8 (z_hi: 4, z_lo: 2; z = z_hi * 2 + z_lo), core: 2. Of those that a mesh axis runs over, the one named last changes fastest.
Arguments:
- normed_input_rows: bfloat16 [2, 8, 4096, 4096], P(None, 'wt', 'seq'), may hold values from -6 to 6
- queries: bfloat16 [2, 8, 4096, 4096], P(None, 'wt', 'seq'), may hold values from -150 to 150
- rotated_key_rows: bfloat16 [2, 8, 4096, 512], P(None, 'wt', 'seq'), may hold values from -6 to 6
- frozen_value_matrix: bfloat16 [4096, 512], P('wt'), may hold values from -0.09375 to 0.09375
- adapter_down_weight: bfloat16 [4096, 8], replicated, may hold values from -0.09375 to 0.09375
- adapter_up_weight: bfloat16 [8, 512], replicated, may hold values from -1.1953125 to 1.1953125
- output_gradient: bfloat16 [2, 8, 4096, 4096], P(None, 'wt', 'seq'), may hold values from -6 to 6
- shifted_head_mask: int32 [32], replicated, may hold values from 0 to 1, as said below
Outputs:
- query_grad: bfloat16 [2, 8, 4096, 4096], P(None, 'wt', 'seq')
- key_grad: bfloat16 [2, 8, 4096, 512], P(None, 'wt', 'seq')
- down_grad: float32 [4096, 8], replicated
- up_grad: float32 [8, 512], replicated
The draws below stay inside these ranges and needn't reach their ends.
Inputs may be any that keep to these rules, and one draw needn't show every extreme that they name: `shifted_head_mask`: exactly half of the 32 query heads are 1; which ones varies.
All inputs are finite; a program needn't handle non-finite values.
Results may differ from the reference program's by a relative error of at most 0.028.
Values may be sent and summed in bfloat16 or wider, within the bound.
No kernel may reach another device: no remote copies, remote signals or barrier semaphores. Data moves between devices by JAX's collectives and lax.ppermute only.
A program may use at most 64 MiB of HBM per device.

```python
import math
import jax
import jax.numpy as jnp
from jax import lax

INPUT_FEATURES = 4096
HEAD_WIDTH = 128
ADAPTER_RANK = 8
GROUP = 1024
SEQS = 2
RANGES = 8
SPAN = 4096
HQ = 32
KEY_VALUE_HEADS = 4


def draw_queries(key, part):
    key = jax.random.fold_in(key, 11)
    base_key = jax.random.fold_in(key, 0)
    full_shape = (SEQS, RANGES, SPAN, HQ, HEAD_WIDTH)
    value_states = jnp.clip(jax.random.normal(base_key, full_shape, jnp.float32), -6.0, 6.0)
    return value_states.reshape(SEQS, RANGES, SPAN, HQ * HEAD_WIDTH).astype(jnp.bfloat16)


def draw_shifted_head_mask(key, part):
    key = jax.random.fold_in(key, 5)
    shuffled = jax.random.permutation(key, HQ)
    return (shuffled < HQ // 2).astype(jnp.int32)


def levels(rng, shape, pieces, least, top_value):
    gain = 1.0
    for axis_at, shards_of in pieces:
        draws = jax.random.uniform(jax.random.fold_in(jax.random.fold_in(rng, 6), axis_at), (shards_of,), jnp.float32, least / len(pieces), top_value / len(pieces))
        gain = gain * jnp.repeat(jnp.exp(draws), shape[axis_at] // shards_of).reshape((-1,) + (1,) * (len(shape) - 1 - axis_at))
    return gain


def normal_values(key, extent, scale, limit, shards=(), kind=jnp.bfloat16):
    entries = jax.random.normal(key, extent, jnp.float32) * scale
    if len(shards) > 0:
        entries = levels(key, extent, shards, -0.22, 0.18) * entries
    return jnp.clip(entries, min=-limit, max=limit).astype(kind)


def setup_inputs(seed: int = 0) -> dict:
    keys = jax.random.split(jax.random.key(seed), 9)
    normed_input_rows = normal_values(keys[0], (SEQS, RANGES, SPAN, INPUT_FEATURES), 1.0, 6.0, ((1, 8), (2, 64)))
    queries = draw_queries(jax.random.fold_in(keys[8], 71), 0)
    rotated_key_rows = normal_values(keys[2], (SEQS, RANGES, SPAN, KEY_VALUE_HEADS * HEAD_WIDTH), 1.0, 6.0, ((1, 8), (2, 64)))
    frozen_value_matrix = normal_values(keys[3], (INPUT_FEATURES, KEY_VALUE_HEADS * HEAD_WIDTH), INPUT_FEATURES ** -0.5, 0.09375, ((0, 8),))
    adapter_down_weight = normal_values(keys[4], (INPUT_FEATURES, ADAPTER_RANK), INPUT_FEATURES ** -0.5, 0.09375)
    adapter_up_weight = normal_values(keys[5], (ADAPTER_RANK, KEY_VALUE_HEADS * HEAD_WIDTH), 0.2, 1.1953125)
    output_gradient = normal_values(keys[6], (SEQS, RANGES, SPAN, HQ * HEAD_WIDTH), 1.0, 6.0, ((1, 8), (2, 64)))
    shifted_head_mask = draw_shifted_head_mask(jax.random.fold_in(keys[8], 71), 0)
    return dict(normed_input_rows=normed_input_rows, queries=queries, rotated_key_rows=rotated_key_rows, frozen_value_matrix=frozen_value_matrix, adapter_down_weight=adapter_down_weight, adapter_up_weight=adapter_up_weight, output_gradient=output_gradient, shifted_head_mask=shifted_head_mask)


adapter_scale = 2.0

def attend_block(query_rows, key_rows, value_rows, grad_rows, offset):
    scale_factor = 1.0 / math.sqrt(query_rows.shape[1])
    scores = jnp.dot(query_rows, key_rows.T, preferred_element_type=jnp.float32) * scale_factor
    query_place = offset + jnp.arange(query_rows.shape[0], dtype=jnp.int32)[:, None]
    key_place = jnp.arange(key_rows.shape[0], dtype=jnp.int32)[None, :]
    scores = jnp.where(key_place <= query_place, scores, -jnp.inf)
    row_max = lax.optimization_barrier(jnp.max(scores, axis=1, keepdims=True))
    raised = jnp.exp(scores - row_max)
    weights = raised / lax.optimization_barrier(jnp.sum(raised, axis=1, keepdims=True))
    rounded = weights.astype(jnp.bfloat16)
    output = jnp.dot(rounded, value_rows, preferred_element_type=jnp.float32)
    deltas = lax.optimization_barrier(jnp.sum(grad_rows.astype(jnp.float32) * output, axis=1, keepdims=True))
    value_grad = jnp.dot(rounded.T, grad_rows, preferred_element_type=jnp.float32)
    weight_grad = jnp.dot(grad_rows, value_rows.T, preferred_element_type=jnp.float32)
    score_grad = (weights * (weight_grad - deltas)).astype(jnp.bfloat16)
    query_grad = jnp.dot(score_grad, key_rows, preferred_element_type=jnp.float32) * scale_factor
    key_grad = jnp.dot(score_grad.T, query_rows, preferred_element_type=jnp.float32) * scale_factor
    return (query_grad, key_grad, value_grad)

def group_grads(stacked):
    middle = stacked.shape[1] // 2
    early_grads = attend_block(stacked[0, :middle], stacked[1, :middle], stacked[2, :middle], stacked[3, :middle], 0)
    later_grads = attend_block(stacked[0, middle:], stacked[1], stacked[2], stacked[3, middle:], middle)
    filler = jnp.zeros((middle, stacked.shape[2]), jnp.float32)
    query_part = jnp.concatenate([early_grads[0], later_grads[0]], axis=0)
    key_part = later_grads[1] + jnp.concatenate([early_grads[1], filler], axis=0)
    value_part = later_grads[2] + jnp.concatenate([early_grads[2], filler], axis=0)
    return jnp.stack([query_part, key_part, value_part]).astype(jnp.bfloat16)

def roll_rows(stacked, amount):
    doubled = jnp.concatenate([stacked, stacked], axis=1)
    return lax.dynamic_slice_in_dim(doubled, amount, stacked.shape[1], 1)

def reference(normed_input_rows, queries, rotated_key_rows, frozen_value_matrix, adapter_down_weight, adapter_up_weight, output_gradient, shifted_head_mask):
    sequences, range_count, span_rows, model_width = normed_input_rows.shape
    head_size = HEAD_WIDTH
    query_heads = queries.shape[3] // head_size
    value_heads = rotated_key_rows.shape[3] // head_size
    group_ratio = query_heads // value_heads
    length = range_count * span_rows
    token_total = sequences * length
    token_positions = normed_input_rows.reshape(token_total, model_width)
    low_rank_rows = jnp.dot(token_positions, adapter_down_weight, preferred_element_type=jnp.float32)
    adapter_up_matrix = adapter_up_weight.astype(jnp.float32)
    adapter_value_term = jnp.dot(low_rank_rows, adapter_up_matrix, precision=lax.Precision.HIGHEST)
    frozen_value_term = jnp.dot(token_positions, frozen_value_matrix, preferred_element_type=jnp.float32)
    value_states = (frozen_value_term + adapter_scale * adapter_value_term).astype(jnp.bfloat16)
    query_seq = queries.reshape(sequences, length, query_heads, head_size)
    key_seq = rotated_key_rows.reshape(sequences, length, value_heads, head_size)
    value_seq = value_states.reshape(sequences, length, value_heads, head_size)
    grad_seq = output_gradient.reshape(sequences, length, query_heads, head_size)
    half_group = GROUP // 2

    def one_group(flat_index):
        sequence = flat_index // value_heads
        value_head = flat_index % value_heads
        key_rows = key_seq[sequence, :, value_head]
        value_rows = value_seq[sequence, :, value_head]

        def one_head(totals, member):
            query_head = value_head * group_ratio + member
            stacked = jnp.stack([query_seq[sequence, :, query_head], key_rows, value_rows, grad_seq[sequence, :, query_head]])
            shifted = lax.dynamic_index_in_dim(shifted_head_mask, query_head, 0, keepdims=False)
            amount = (shifted * half_group).astype(jnp.int32)
            working = roll_rows(stacked, amount)
            blocks = jnp.transpose(working.reshape(4, length // GROUP, GROUP, head_size), (1, 0, 2, 3))
            gradients = lax.map(group_grads, blocks)
            gradients = jnp.transpose(gradients, (1, 0, 2, 3)).reshape(3, length, head_size)
            gradients = roll_rows(gradients, (length - amount).astype(jnp.int32))
            totals = (totals[0] + gradients[1].astype(jnp.float32), totals[1] + gradients[2].astype(jnp.float32))
            return (totals, gradients[0])
        zeros = jnp.zeros((length, head_size), jnp.float32)
        totals, query_grads = lax.scan(one_head, (zeros, zeros), jnp.arange(group_ratio, dtype=jnp.int32))
        return (query_grads, totals[0].astype(jnp.bfloat16), totals[1])
    query_all, key_all, value_all = lax.map(one_group, jnp.arange(sequences * value_heads, dtype=jnp.int32))
    query_grad = jnp.transpose(query_all.reshape(sequences, query_heads, length, head_size), (0, 2, 1, 3))
    query_grad = query_grad.reshape(sequences, range_count, span_rows, query_heads * head_size)
    key_grad = jnp.transpose(key_all.reshape(sequences, value_heads, length, head_size), (0, 2, 1, 3))
    key_grad = key_grad.reshape(sequences, range_count, span_rows, value_heads * head_size)
    value_grad = jnp.transpose(value_all.reshape(sequences, value_heads, length, head_size), (0, 2, 1, 3))
    value_grad = value_grad.reshape(token_total, value_heads * head_size)
    pulled = jnp.dot(value_grad, adapter_up_matrix.T, precision=lax.Precision.HIGHEST).astype(jnp.bfloat16)
    scale_factor = adapter_scale / math.sqrt(token_total)
    down_grad = jnp.dot(token_positions.T, pulled, preferred_element_type=jnp.float32) * scale_factor
    up_grad = jnp.dot(low_rank_rows.T, value_grad, precision=lax.Precision.HIGHEST) * scale_factor
    return (query_grad, key_grad, down_grad, up_grad)
```

```python
import math

import jax
import jax.numpy as jnp
from jax import lax
from jax.experimental import pallas as pl
from jax.experimental.pallas import tpu as pltpu
from jax.sharding import PartitionSpec as P

HEAD = 128
HALF = 512
TILE = 256
RATIO = 8
KV = 4
RANK = 8
UNITS = 8
SCALE = 1.0 / math.sqrt(HEAD)
ADAPTER_SCALE = 2.0
VMEM = 48 * 1024 * 1024
F32 = jnp.float32
BF16 = jnp.bfloat16


def dot_nt(a, b):
    return lax.dot_general(a, b, (((1,), (1,)), ((), ())), preferred_element_type=F32)


def dot_nn(a, b):
    return lax.dot_general(a, b, (((1,), (0,)), ((), ())), preferred_element_type=F32)


def weights_kernel(flags, q_ref, k_ref, kp_ref, p_ref):
    head = pl.program_id(0)
    factor = SCALE * math.log2(math.e)

    def tiles(full):
        for r in range(HALF // TILE):
            cols = pl.ds(r * TILE, TILE)
            keys = (r + 1) * TILE
            q = q_ref[cols, :]
            own = dot_nt(k_ref[pl.ds(0, keys), :], q)
            key_place = lax.broadcasted_iota(jnp.int32, (keys, TILE), 0)
            query_place = lax.broadcasted_iota(jnp.int32, (keys, TILE), 1) + r * TILE
            own = jnp.where(key_place <= query_place, own, -jnp.inf)
            top = jnp.max(own, axis=0, keepdims=True)
            if full:
                prev = dot_nt(kp_ref[...], q)
                top = jnp.maximum(top, jnp.max(prev, axis=0, keepdims=True))
            own = jnp.exp2((own - top) * factor)
            total = jnp.sum(own, axis=0, keepdims=True)
            if full:
                prev = jnp.exp2((prev - top) * factor)
                total = total + jnp.sum(prev, axis=0, keepdims=True)
            inverse = 1.0 / total
            p_ref[0, pl.ds(HALF, keys), cols] = (own * inverse).astype(BF16)
            if full:
                p_ref[0, pl.ds(0, HALF), cols] = (prev * inverse).astype(BF16)

    @pl.when(flags[head] > 0)
    def _():
        tiles(True)

    @pl.when(flags[head] == 0)
    def _():
        tiles(False)


def value_grad_kernel(flags, p_ref, do_ref, out_ref, acc):
    head = pl.program_id(0)

    @pl.when(head == 0)
    def _():
        acc[...] = jnp.zeros_like(acc)

    acc[pl.ds(HALF, TILE), :] += dot_nn(p_ref[0, pl.ds(HALF, TILE), :], do_ref[...])
    acc[pl.ds(HALF + TILE, TILE), :] += dot_nn(
        p_ref[0, pl.ds(HALF + TILE, TILE), pl.ds(TILE, TILE)], do_ref[pl.ds(TILE, TILE), :]
    )

    @pl.when(flags[head] > 0)
    def _():
        acc[pl.ds(0, HALF), :] += dot_nn(p_ref[0, pl.ds(0, HALF), :], do_ref[...])

    @pl.when(head == RATIO - 1)
    def _():
        out_ref[:, pl.ds(0, HEAD)] = acc[pl.ds(HALF, HALF), :].astype(BF16)
        out_ref[:, pl.ds(HEAD, HEAD)] = acc[pl.ds(0, HALF), :].astype(BF16)


def score_grad_kernel(flags, p_ref, q_ref, k_ref, kp_ref, do_ref, v_ref, out_ref, acc, kt):
    head = pl.program_id(0)

    @pl.when(head == 0)
    def _():
        acc[...] = jnp.zeros_like(acc)
        kt[:, pl.ds(0, HALF)] = kp_ref[...].astype(F32).T.astype(BF16)
        kt[:, pl.ds(HALF, HALF)] = k_ref[...].astype(F32).T.astype(BF16)

    def tiles(full):
        for r in range(HALF // TILE):
            cols = pl.ds(r * TILE, TILE)
            keys = (r + 1) * TILE
            q = q_ref[cols, :]
            do = do_ref[cols, :]
            p_own = p_ref[0, pl.ds(HALF, keys), cols].astype(F32)
            d_own = dot_nt(v_ref[pl.ds(0, keys), pl.ds(0, HEAD)], do)
            delta = jnp.sum(p_own * d_own, axis=0, keepdims=True)
            if full:
                p_prev = p_ref[0, pl.ds(0, HALF), cols].astype(F32)
                d_prev = dot_nt(v_ref[:, pl.ds(HEAD, HEAD)], do)
                delta = delta + jnp.sum(p_prev * d_prev, axis=0, keepdims=True)
            s_own = (p_own * (d_own - delta)).astype(BF16)
            dq = dot_nn(kt[:, pl.ds(HALF, keys)], s_own)
            acc[pl.ds(HALF, keys), :] += dot_nn(s_own, q)
            if full:
                s_prev = (p_prev * (d_prev - delta)).astype(BF16)
                dq = dq + dot_nn(kt[:, pl.ds(0, HALF)], s_prev)
                acc[pl.ds(0, HALF), :] += dot_nn(s_prev, q)
            place = pl.ds(pl.multiple_of(head * HEAD, HEAD), HEAD)
            out_ref[cols, place] = (dq * SCALE).T.astype(BF16)

    @pl.when(flags[head] > 0)
    def _():
        tiles(True)

    @pl.when(flags[head] == 0)
    def _():
        tiles(False)

    @pl.when(head == RATIO - 1)
    def _():
        out_ref[:, pl.ds(RATIO * HEAD, HEAD)] = (acc[pl.ds(HALF, HALF), :] * SCALE).astype(BF16)
        out_ref[:, pl.ds((RATIO + 1) * HEAD, HEAD)] = (acc[pl.ds(0, HALF), :] * SCALE).astype(BF16)


def values_kernel(x_ref, xh_ref, w_ref, low_ref, up_ref, out_ref, acc):
    step = pl.program_id(0)
    rows = x_ref.shape[0]

    @pl.when(step == 0)
    def _():
        up = up_ref[...].astype(F32)
        acc[...] = ADAPTER_SCALE * lax.dot_general(
            low_ref[...],
            up,
            (((1,), (0,)), ((), ())),
            preferred_element_type=F32,
            precision=lax.Precision.HIGHEST,
        )

    acc[pl.ds(0, rows), :] += dot_nn(x_ref[...], w_ref[...])
    acc[pl.ds(rows, rows), :] += dot_nn(xh_ref[...], w_ref[...])

    @pl.when(step == pl.num_programs(0) - 1)
    def _():
        part = rows // 2
        for s in range(2):
            for g in range(KV):
                for o in range(2):
                    out_ref[s * KV + g, :, pl.ds(o * HEAD, HEAD)] = acc[
                        pl.ds(o * rows + s * part, part), pl.ds(g * HEAD, HEAD)
                    ].astype(BF16)


def adapter_kernel(dv_ref, x_ref, xh_ref, low_ref, up_ref, out_ref):
    rows = x_ref.shape[0]
    width = x_ref.shape[1]
    part = rows // 2
    down = jnp.zeros((RANK, width), F32)
    for o, source in enumerate((x_ref, xh_ref)):
        for s in range(2):
            pulled = jnp.zeros((RANK, part), F32)
            for g in range(KV):
                block = dv_ref[s * KV + g, :, pl.ds(o * HEAD, HEAD)]
                pulled = pulled + dot_nt(up_ref[:, pl.ds(g * HEAD, HEAD)], block)
            down = down + dot_nn(pulled.astype(BF16), source[pl.ds(s * part, part), :])
    for c in range(width // HEAD):
        out_ref[pl.ds(c * RANK, RANK), :] = down[:, c * HEAD : (c + 1) * HEAD]
    base = width // HEAD
    for g in range(KV):
        up = jnp.zeros((RANK, HEAD), F32)
        for o in range(2):
            for s in range(2):
                block = dv_ref[s * KV + g, :, pl.ds(o * HEAD, HEAD)].astype(F32)
                up = up + lax.dot_general(
                    low_ref[o * 2 + s],
                    block,
                    (((1,), (0,)), ((), ())),
                    preferred_element_type=F32,
                    precision=lax.Precision.HIGHEST,
                )
        out_ref[pl.ds((base + g) * RANK, RANK), :] = up
    used = (base + KV) * RANK
    if out_ref.shape[0] > used:
        out_ref[pl.ds(used, out_ref.shape[0] - used), :] = jnp.zeros(
            (out_ref.shape[0] - used, HEAD), F32
        )


def call(kernel, flops, nbytes, **keywords):
    return pl.pallas_call(
        kernel,
        compiler_params=pltpu.CompilerParams(vmem_limit_bytes=VMEM),
        cost_estimate=pl.CostEstimate(flops=flops, bytes_accessed=nbytes, transcendentals=0),
        **keywords,
    )


def body(x, queries, keys, frozen, down_weight, up_weight, grads, mask):
    seq_devices = lax.axis_size("seq")
    weight_devices = lax.axis_size("wt")
    devices = seq_devices * weight_devices
    sequences, _, rows, width = x.shape
    tokens = sequences * rows
    y_planes = seq_devices // UNITS
    both = ("seq", "wt")
    groups = [[UNITS * y + j for j in range(UNITS)] for y in range(y_planes)]
    smem = pl.BlockSpec(memory_space=pltpu.SMEM)

    from_before = []
    for y in range(y_planes):
        for j in range(UNITS):
            for w in range(weight_devices):
                source = (y * UNITS + j) * weight_devices + w
                ny, nw = (y + 1, w) if y + 1 < y_planes else (0, (w + 1) % weight_devices)
                from_before.append((source, (ny * UNITS + j) * weight_devices + nw))
    to_before = [(b, a) for a, b in from_before]

    def swap(block):
        return lax.all_to_all(
            block, "seq", split_axis=0, concat_axis=0, axis_index_groups=groups, tiled=True
        )

    def by_unit(source, columns):
        split = source.reshape(sequences, rows, KV, columns)
        return jnp.transpose(split, (0, 2, 1, 3)).reshape(UNITS, rows, columns)

    place = lax.axis_index("seq")
    parity = (place // UNITS) % 2
    kv_head = place % KV
    my_mask = lax.dynamic_slice_in_dim(mask, kv_head * RATIO, RATIO, 0)
    flags = jnp.where(parity == 1, 1 - my_mask, my_mask).astype(jnp.int32)

    x_rows = x.reshape(tokens, width)
    wide = RATIO * HEAD

    first = swap(jnp.concatenate([by_unit(queries, wide), by_unit(keys, HEAD)], axis=2))
    second_in = by_unit(grads, wide)
    second_in, first = lax.optimization_barrier((second_in, first))
    second = swap(second_in)
    first = first.reshape(HALF, wide + HEAD)
    do_unit = second.reshape(HALF, wide)
    k_prev = lax.ppermute(first[:, wide:], both, from_before)
    x_before = lax.ppermute(x_rows, both, from_before)
    frozen_all = lax.all_gather(frozen, "wt", axis=0, tiled=True)

    head_block = pl.BlockSpec((HALF, HEAD), lambda h: (0, h))
    key_block = pl.BlockSpec((HALF, HEAD), lambda h: (0, RATIO))
    prev_block = pl.BlockSpec((HALF, HEAD), lambda h: (0, 0))
    p_block = pl.BlockSpec((1, 2 * HALF, HALF), lambda h: (h, 0, 0))

    product = 2 * RATIO * HALF * HALF * 3 // 2 * HEAD
    weights = call(
        weights_kernel,
        product,
        10 << 20,
        grid=(RATIO,),
        in_specs=[smem, head_block, key_block, prev_block],
        out_specs=p_block,
        out_shape=jax.ShapeDtypeStruct((RATIO, 2 * HALF, HALF), BF16),
        name="weights",
    )(flags, first, first, k_prev)

    dv_unit = call(
        value_grad_kernel,
        product,
        10 << 20,
        grid=(RATIO,),
        in_specs=[smem, p_block, head_block],
        out_specs=pl.BlockSpec((HALF, 2 * HEAD), lambda h: (0, 0)),
        out_shape=jax.ShapeDtypeStruct((HALF, 2 * HEAD), BF16),
        scratch_shapes=[pltpu.VMEM((2 * HALF, HEAD), F32)],
        name="value_grad",
    )(flags, weights, do_unit)
    dv_tokens = swap(dv_unit.reshape(UNITS, rows, 2 * HEAD))

    low = jnp.concatenate(
        [
            jnp.dot(x_rows, down_weight, preferred_element_type=F32),
            jnp.dot(x_before, down_weight, preferred_element_type=F32),
        ],
        axis=0,
    )
    low_parts = jnp.transpose(low.reshape(4, rows, RANK), (0, 2, 1))

    chunks = (width // HEAD + KV) * RANK
    share = -(-chunks // devices)
    whole = share * devices
    sums = call(
        adapter_kernel,
        4 * tokens * width * RANK,
        3 << 20,
        out_shape=jax.ShapeDtypeStruct((whole, HEAD), F32),
        name="adapter",
    )(dv_tokens, x_rows, x_before, low_parts, up_weight)
    scattered = lax.all_to_all(sums, both, split_axis=0, concat_axis=0, tiled=True)
    mine = jnp.sum(scattered.reshape(devices, share, HEAD), axis=0)
    mine = mine * (ADAPTER_SCALE / math.sqrt(tokens * devices))
    spread = jnp.broadcast_to(mine[None], (devices, share, HEAD)).reshape(whole, HEAD)
    gathered = lax.all_to_all(spread, both, split_axis=0, concat_axis=0, tiled=True)
    down_rows = gathered[: width // HEAD * RANK].reshape(width // HEAD, RANK, HEAD)
    down_grad = jnp.transpose(down_rows, (0, 2, 1)).reshape(width, RANK)
    up_rows = gathered[width // HEAD * RANK : chunks].reshape(KV, RANK, HEAD)
    up_grad = jnp.transpose(up_rows, (1, 0, 2)).reshape(RANK, KV * HEAD)

    steps = 4
    values = call(
        values_kernel,
        4 * tokens * width * KV * HEAD,
        6 << 20,
        grid=(steps,),
        in_specs=[
            pl.BlockSpec((tokens, width // steps), lambda i: (0, i)),
            pl.BlockSpec((tokens, width // steps), lambda i: (0, i)),
            pl.BlockSpec((width // steps, KV * HEAD), lambda i: (i, 0)),
            pl.BlockSpec((2 * tokens, RANK), lambda i: (0, 0)),
            pl.BlockSpec((RANK, KV * HEAD), lambda i: (0, 0)),
        ],
        out_specs=pl.BlockSpec((UNITS, rows, 2 * HEAD), lambda i: (0, 0, 0)),
        out_shape=jax.ShapeDtypeStruct((UNITS, rows, 2 * HEAD), BF16),
        scratch_shapes=[pltpu.VMEM((2 * tokens, KV * HEAD), F32)],
        name="values",
    )(x_rows, x_before, frozen_all, low, up_weight)
    v_unit = swap(values).reshape(HALF, 2 * HEAD)

    total = (RATIO + 2) * HEAD
    unit_grads = call(
        score_grad_kernel,
        3 * product,
        12 << 20,
        grid=(RATIO,),
        in_specs=[
            smem,
            p_block,
            head_block,
            key_block,
            prev_block,
            head_block,
            pl.BlockSpec((HALF, 2 * HEAD), lambda h: (0, 0)),
        ],
        out_specs=pl.BlockSpec((HALF, total), lambda h: (0, 0)),
        out_shape=jax.ShapeDtypeStruct((HALF, total), BF16),
        scratch_shapes=[pltpu.VMEM((2 * HALF, HEAD), F32), pltpu.VMEM((HEAD, 2 * HALF), BF16)],
        name="score_grad",
    )(flags, weights, first, first, k_prev, do_unit, v_unit)
    returned = swap(unit_grads.reshape(UNITS, rows, total))

    def by_token(part, columns):
        split = jnp.transpose(part.reshape(sequences, KV, rows, columns), (0, 2, 1, 3))
        return split.reshape(sequences, 1, rows, KV * columns)

    query_grad = by_token(returned[:, :, :wide], wide)
    key_own = by_token(returned[:, :, wide : wide + HEAD], HEAD)
    key_before = lax.ppermute(by_token(returned[:, :, wide + HEAD :], HEAD), both, to_before)
    key_grad = (key_own.astype(F32) + key_before.astype(F32)).astype(BF16)
    return (query_grad, key_grad, down_grad, up_grad)


def solution(mesh):
    tokens = P(None, "wt", "seq", None)
    return jax.shard_map(
        body,
        mesh=mesh,
        in_specs=(tokens, tokens, tokens, P("wt", None), P(), P(), tokens, P()),
        out_specs=(tokens, tokens, P(), P()),
        check_vma=False,
    )
```

```python
import functools
import math

import jax
import jax.numpy as jnp
from jax import lax
from jax.experimental import pallas as pl
from jax.experimental.pallas import tpu as pltpu
from jax.sharding import PartitionSpec as P

HEAD = 128
HALF = 512
TILE = 256
RATIO = 8
KV = 4
RANK = 8
UNITS = 8
SCALE = 1.0 / math.sqrt(HEAD)
ADAPTER_SCALE = 2.0
VMEM = 48 * 1024 * 1024
F32 = jnp.float32
BF16 = jnp.bfloat16


def dot_nt(a, b):
    return lax.dot_general(a, b, (((1,), (1,)), ((), ())), preferred_element_type=F32)


def dot_nn(a, b):
    return lax.dot_general(a, b, (((1,), (0,)), ((), ())), preferred_element_type=F32)


def weights_kernel(flags, q_ref, k_ref, kp_ref, own_ref, prev_ref):
    head = pl.program_id(0)
    factor = SCALE * math.log2(math.e)

    def tiles(full):
        for r in range(HALF // TILE):
            cols = pl.ds(r * TILE, TILE)
            q = q_ref[cols, :]
            key_place = lax.broadcasted_iota(jnp.int32, (TILE, TILE), 0)
            query_place = lax.broadcasted_iota(jnp.int32, (TILE, TILE), 1)
            scores = dot_nt(k_ref[cols, :], q)
            scores = jnp.where(key_place <= query_place, scores, -jnp.inf)
            parts = [(own_ref, r * TILE, scores)]
            sources = [(own_ref, k_ref, t) for t in range(r)]
            if full:
                sources += [(prev_ref, kp_ref, t) for t in range(HALF // TILE)]
            for place, keys, t in sources:
                parts.append((place, t * TILE, dot_nt(keys[pl.ds(t * TILE, TILE), :], q)))
            top = functools.reduce(
                jnp.maximum, [jnp.max(scores, axis=0, keepdims=True) for _, _, scores in parts]
            )
            raised = [
                (place, at, jnp.exp2((scores - top) * factor)) for place, at, scores in parts
            ]
            total = sum(jnp.sum(e, axis=0, keepdims=True) for _, _, e in raised)
            inverse = 1.0 / total
            for place, at, e in raised:
                place[0, pl.ds(at, TILE), cols] = (e * inverse).astype(BF16)

    @pl.when(flags[head] > 0)
    def _():
        tiles(True)

    @pl.when(flags[head] == 0)
    def _():
        tiles(False)


def value_grad_kernel(flags, own_ref, prev_ref, do_ref, dv_ref, dvp_ref, acc):
    head = pl.program_id(0)

    @pl.when(head == 0)
    def _():
        acc[...] = jnp.zeros_like(acc)

    acc[pl.ds(HALF, TILE), :] += dot_nn(own_ref[0, pl.ds(0, TILE), :], do_ref[...])
    acc[pl.ds(HALF + TILE, TILE), :] += dot_nn(
        own_ref[0, pl.ds(TILE, TILE), pl.ds(TILE, TILE)], do_ref[pl.ds(TILE, TILE), :]
    )

    @pl.when(flags[head] > 0)
    def _():
        acc[pl.ds(0, HALF), :] += dot_nn(prev_ref[0], do_ref[...])

    @pl.when(head == RATIO - 1)
    def _():
        dv_ref[...] = acc[pl.ds(HALF, HALF), :]
        dvp_ref[...] = acc[pl.ds(0, HALF), :].astype(BF16)


def score_grad_kernel(
    flags, own_ref, prev_ref, q_ref, k_ref, kp_ref, do_ref, v_ref, vp_ref, out_ref, acc, kt
):
    head = pl.program_id(0)

    @pl.when(head == 0)
    def _():
        acc[...] = jnp.zeros_like(acc)
        kt[:, pl.ds(0, HALF)] = kp_ref[...].astype(F32).T.astype(BF16)
        kt[:, pl.ds(HALF, HALF)] = k_ref[...].astype(F32).T.astype(BF16)

    def tiles(full):
        for r in range(HALF // TILE):
            cols = pl.ds(r * TILE, TILE)
            q = q_ref[cols, :]
            do = do_ref[cols, :]
            sources = [(own_ref, v_ref, t * TILE, HALF) for t in range(r + 1)]
            if full:
                sources += [(prev_ref, vp_ref, t * TILE, 0) for t in range(HALF // TILE)]
            parts = []
            for place, values, at, base in sources:
                p = place[0, pl.ds(at, TILE), cols].astype(F32)
                parts.append((p, dot_nt(values[pl.ds(at, TILE), :], do), at + base))
            delta = sum(jnp.sum(p * d, axis=0, keepdims=True) for p, d, _ in parts)
            dq = jnp.zeros((HEAD, TILE), F32)
            for p, d, at in parts:
                score_grad = (p * (d - delta)).astype(BF16)
                dq = dq + dot_nn(kt[:, pl.ds(at, TILE)], score_grad)
                acc[pl.ds(at, TILE), :] += dot_nn(score_grad, q)
            place = pl.ds(pl.multiple_of(head * HEAD, HEAD), HEAD)
            out_ref[cols, place] = (dq * SCALE).T.astype(BF16)

    @pl.when(flags[head] > 0)
    def _():
        tiles(True)

    @pl.when(flags[head] == 0)
    def _():
        tiles(False)

    @pl.when(head == RATIO - 1)
    def _():
        out_ref[:, pl.ds(RATIO * HEAD, HEAD)] = (acc[pl.ds(HALF, HALF), :] * SCALE).astype(BF16)
        out_ref[:, pl.ds((RATIO + 1) * HEAD, HEAD)] = (acc[pl.ds(0, HALF), :] * SCALE).astype(BF16)


def values_kernel(x_ref, xo_ref, w_ref, low_ref, up_ref, own_ref, other_ref, acc):
    step = pl.program_id(0)
    rows = x_ref.shape[0]

    @pl.when(step == 0)
    def _():
        acc[...] = ADAPTER_SCALE * lax.dot_general(
            low_ref[...],
            up_ref[...].astype(F32),
            (((1,), (0,)), ((), ())),
            preferred_element_type=F32,
            precision=lax.Precision.HIGHEST,
        )

    acc[pl.ds(0, rows), :] += dot_nn(x_ref[...], w_ref[...])
    acc[pl.ds(rows, rows), :] += dot_nn(xo_ref[...], w_ref[...])

    @pl.when(step == pl.num_programs(0) - 1)
    def _():
        own_ref[...] = acc[pl.ds(0, rows), :].astype(BF16)
        other_ref[...] = acc[pl.ds(rows, rows), :].astype(BF16)


def adapter_kernel(dv_ref, x_ref, low_ref, up_ref, out_ref):
    width = x_ref.shape[1]
    part = x_ref.shape[0] // 2
    down = jnp.zeros((RANK, width), F32)
    for s in range(2):
        pulled = jnp.zeros((RANK, part), F32)
        for g in range(KV):
            pulled = pulled + dot_nt(up_ref[:, pl.ds(g * HEAD, HEAD)], dv_ref[s * KV + g])
        down = down + dot_nn(pulled.astype(BF16), x_ref[pl.ds(s * part, part), :])
    for c in range(width // HEAD):
        out_ref[pl.ds(c * RANK, RANK), :] = down[:, c * HEAD : (c + 1) * HEAD]
    base = width // HEAD
    for g in range(KV):
        up = jnp.zeros((RANK, HEAD), F32)
        for s in range(2):
            up = up + lax.dot_general(
                low_ref[s],
                dv_ref[s * KV + g].astype(F32),
                (((1,), (0,)), ((), ())),
                preferred_element_type=F32,
                precision=lax.Precision.HIGHEST,
            )
        out_ref[pl.ds((base + g) * RANK, RANK), :] = up
    used = (base + KV) * RANK
    if out_ref.shape[0] > used:
        out_ref[pl.ds(used, out_ref.shape[0] - used), :] = jnp.zeros(
            (out_ref.shape[0] - used, HEAD), F32
        )


def call(kernel, flops, nbytes, **keywords):
    return pl.pallas_call(
        kernel,
        compiler_params=pltpu.CompilerParams(vmem_limit_bytes=VMEM),
        cost_estimate=pl.CostEstimate(flops=flops, bytes_accessed=nbytes, transcendentals=0),
        **keywords,
    )


def body(x, queries, keys, frozen, down_weight, up_weight, grads, mask):
    seq_devices = lax.axis_size("seq")
    weight_devices = lax.axis_size("wt")
    devices = seq_devices * weight_devices
    sequences, _, rows, width = x.shape
    tokens = sequences * rows
    y_planes = seq_devices // UNITS
    both = ("seq", "wt")
    groups = [[UNITS * y + j for j in range(UNITS)] for y in range(y_planes)]
    smem = pl.BlockSpec(memory_space=pltpu.SMEM)

    def flat(y, j, w):
        return (y * UNITS + j) * weight_devices + w

    everywhere = [
        (y, j, w) for y in range(y_planes) for j in range(UNITS) for w in range(weight_devices)
    ]
    from_before = [
        (
            flat(y, j, w),
            flat(y + 1, j, w) if y + 1 < y_planes else flat(0, j, (w + 1) % weight_devices),
        )
        for y, j, w in everywhere
    ]
    to_before = [(b, a) for a, b in from_before]
    turned = [(flat(w, j, y), flat(y, j, w)) for y, j, w in everywhere]
    other_core = [(w, w ^ 1) for w in range(weight_devices)]
    columns_of_y = [[UNITS * y + j for y in range(y_planes)] for j in range(UNITS)]

    def swap(block):
        return lax.all_to_all(
            block, "seq", split_axis=0, concat_axis=0, axis_index_groups=groups, tiled=True
        )

    def by_unit(source, columns):
        split = source.reshape(sequences, rows, KV, columns)
        return jnp.transpose(split, (0, 2, 1, 3)).reshape(UNITS, rows, columns)

    place = lax.axis_index("seq")
    parity = (place // UNITS) % 2
    kv_head = place % KV
    my_mask = lax.dynamic_slice_in_dim(mask, kv_head * RATIO, RATIO, 0)
    flags = jnp.where(parity == 1, 1 - my_mask, my_mask).astype(jnp.int32)

    x_rows = x.reshape(tokens, width)
    wide = RATIO * HEAD
    core = lax.axis_index("wt") % 2
    half_columns = KV * HEAD // 2

    shard = lax.dynamic_slice_in_dim(frozen, (place // UNITS) % 2 * half_columns, half_columns, 1)
    shard = lax.ppermute(shard, both, turned)
    frozen_half = lax.all_gather(
        shard, "seq", axis=0, axis_index_groups=columns_of_y, tiled=True
    )
    x_other = lax.ppermute(x_rows, "wt", other_core)

    first = swap(jnp.concatenate([by_unit(queries, wide), by_unit(keys, HEAD)], axis=2))
    second_in = by_unit(grads, wide)
    second_in, first = lax.optimization_barrier((second_in, first))
    second = swap(second_in)
    first = first.reshape(HALF, wide + HEAD)
    do_unit = second.reshape(HALF, wide)
    k_prev = lax.ppermute(first[:, wide:], both, from_before)

    head_block = pl.BlockSpec((HALF, HEAD), lambda h: (0, h))
    key_block = pl.BlockSpec((HALF, HEAD), lambda h: (0, RATIO))
    prev_block = pl.BlockSpec((HALF, HEAD), lambda h: (0, 0))
    p_block = pl.BlockSpec((1, HALF, HALF), lambda h: (h, 0, 0))
    p_shape = pltpu.HBM((RATIO, HALF, HALF), BF16)

    product = 2 * RATIO * HALF * HALF * 3 // 2 * HEAD
    weights_own, weights_prev = call(
        weights_kernel,
        product,
        10 << 20,
        grid=(RATIO,),
        in_specs=[smem, head_block, key_block, prev_block],
        out_specs=(p_block, p_block),
        out_shape=(p_shape, p_shape),
        name="weights",
    )(flags, first, first, k_prev)
    weights_own = pltpu.with_memory_space_constraint(weights_own, pltpu.HBM)
    weights_prev = pltpu.with_memory_space_constraint(weights_prev, pltpu.HBM)

    dv_own, dv_prev = call(
        value_grad_kernel,
        product,
        10 << 20,
        grid=(RATIO,),
        in_specs=[smem, p_block, p_block, head_block],
        out_specs=(prev_block, prev_block),
        out_shape=(
            jax.ShapeDtypeStruct((HALF, HEAD), F32),
            jax.ShapeDtypeStruct((HALF, HEAD), BF16),
        ),
        scratch_shapes=[pltpu.VMEM((2 * HALF, HEAD), F32)],
        name="value_grad",
    )(flags, weights_own, weights_prev, do_unit)
    dv_next = lax.ppermute(dv_prev, both, to_before)
    dv_unit = (dv_own + dv_next.astype(F32)).astype(BF16).reshape(UNITS, rows, HEAD)

    low = jnp.dot(x_rows, down_weight, preferred_element_type=F32)
    low_other = jnp.dot(x_other, down_weight, preferred_element_type=F32)
    low_parts = jnp.transpose(low.reshape(sequences, rows, RANK), (0, 2, 1))
    up_half = lax.dynamic_slice_in_dim(up_weight, core * half_columns, half_columns, 1)

    steps = 4
    slab = pl.BlockSpec((tokens, width // steps), lambda i: (0, i))
    value_block = pl.BlockSpec((tokens, half_columns), lambda i: (0, 0))
    value_shape = jax.ShapeDtypeStruct((tokens, half_columns), BF16)
    values_mine, values_other = call(
        values_kernel,
        4 * tokens * width * half_columns,
        4 << 20,
        grid=(steps,),
        in_specs=[
            slab,
            slab,
            pl.BlockSpec((width // steps, half_columns), lambda i: (i, 0)),
            pl.BlockSpec((2 * tokens, RANK), lambda i: (0, 0)),
            pl.BlockSpec((RANK, half_columns), lambda i: (0, 0)),
        ],
        out_specs=(value_block, value_block),
        out_shape=(value_shape, value_shape),
        scratch_shapes=[pltpu.VMEM((2 * tokens, half_columns), F32)],
        name="values",
    )(x_rows, x_other, frozen_half, jnp.concatenate([low, low_other], axis=0), up_half)
    values_back = lax.ppermute(values_other, "wt", other_core)
    low_half = jnp.where(core == 0, values_mine, values_back)
    high_half = jnp.where(core == 0, values_back, values_mine)
    value_parts = by_unit(jnp.concatenate([low_half, high_half], axis=1), HEAD)

    third = swap(jnp.concatenate([dv_unit, value_parts], axis=2))
    third_rows = third.reshape(HALF, 2 * HEAD)
    v_prev = lax.ppermute(third_rows[:, HEAD:], both, from_before)

    chunks = (width // HEAD + KV) * RANK
    share = -(-chunks // devices)
    whole = share * devices
    sums = call(
        adapter_kernel,
        4 * tokens * width * RANK,
        3 << 20,
        grid=(1,),
        in_specs=[
            pl.BlockSpec((UNITS, rows, HEAD), lambda i: (0, 0, 0)),
            pl.BlockSpec((tokens, width), lambda i: (0, 0)),
            pl.BlockSpec((sequences, RANK, rows), lambda i: (0, 0, 0)),
            pl.BlockSpec((RANK, KV * HEAD), lambda i: (0, 0)),
        ],
        out_specs=pl.BlockSpec((whole, HEAD), lambda i: (0, 0)),
        out_shape=jax.ShapeDtypeStruct((whole, HEAD), F32),
        name="adapter",
    )(third, x_rows, low_parts, up_weight)
    scattered = lax.all_to_all(sums, both, split_axis=0, concat_axis=0, tiled=True)
    mine = jnp.sum(scattered.reshape(devices, share, HEAD), axis=0)
    mine = mine * (ADAPTER_SCALE / math.sqrt(tokens * devices))
    spread = jnp.broadcast_to(mine[None], (devices, share, HEAD)).reshape(whole, HEAD)
    gathered = lax.all_to_all(spread, both, split_axis=0, concat_axis=0, tiled=True)
    down_rows = gathered[: width // HEAD * RANK].reshape(width // HEAD, RANK, HEAD)
    down_grad = jnp.transpose(down_rows, (0, 2, 1)).reshape(width, RANK)
    up_rows = gathered[width // HEAD * RANK : chunks].reshape(KV, RANK, HEAD)
    up_grad = jnp.transpose(up_rows, (1, 0, 2)).reshape(RANK, KV * HEAD)

    total = (RATIO + 2) * HEAD
    unit_grads = call(
        score_grad_kernel,
        3 * product,
        12 << 20,
        grid=(RATIO,),
        in_specs=[
            smem,
            p_block,
            p_block,
            head_block,
            key_block,
            prev_block,
            head_block,
            pl.BlockSpec((HALF, HEAD), lambda h: (0, 1)),
            prev_block,
        ],
        out_specs=pl.BlockSpec((HALF, total), lambda h: (0, 0)),
        out_shape=jax.ShapeDtypeStruct((HALF, total), BF16),
        scratch_shapes=[pltpu.VMEM((2 * HALF, HEAD), F32), pltpu.VMEM((HEAD, 2 * HALF), BF16)],
        name="score_grad",
    )(
        flags,
        weights_own,
        weights_prev,
        first,
        first,
        k_prev,
        do_unit,
        third_rows,
        v_prev,
    )
    returned = swap(unit_grads.reshape(UNITS, rows, total))

    def by_token(part, columns):
        split = jnp.transpose(part.reshape(sequences, KV, rows, columns), (0, 2, 1, 3))
        return split.reshape(sequences, 1, rows, KV * columns)

    query_grad = by_token(returned[:, :, :wide], wide)
    key_own = by_token(returned[:, :, wide : wide + HEAD], HEAD)
    key_before = lax.ppermute(by_token(returned[:, :, wide + HEAD :], HEAD), both, to_before)
    key_grad = (key_own.astype(F32) + key_before.astype(F32)).astype(BF16)
    return (query_grad, key_grad, down_grad, up_grad)


def solution(mesh):
    tokens = P(None, "wt", "seq", None)
    return jax.shard_map(
        body,
        mesh=mesh,
        in_specs=(tokens, tokens, tokens, P("wt", None), P(), P(), tokens, P()),
        out_specs=(tokens, tokens, P(), P()),
        check_vma=False,
    )
```

```python
import functools
import math

import jax
import jax.numpy as jnp
from jax import lax
from jax.experimental import pallas as pl
from jax.experimental.pallas import tpu as pltpu
from jax.sharding import PartitionSpec as P

HEAD = 128
HALF = 512
TILE = 256
RATIO = 8
KV = 4
RANK = 8
UNITS = 8
PLANES = 8
SHARD = 512
ROWS = 64
SCALE = 1.0 / math.sqrt(HEAD)
ADAPTER_SCALE = 2.0
VMEM = 48 * 1024 * 1024
F32 = jnp.float32
BF16 = jnp.bfloat16


def dot_nt(a, b):
    return lax.dot_general(a, b, (((1,), (1,)), ((), ())), preferred_element_type=F32)


def dot_nn(a, b):
    return lax.dot_general(a, b, (((1,), (0,)), ((), ())), preferred_element_type=F32)


def weights_kernel(
    flags, q_ref, k_ref, kp_ref, do_ref, own_ref, prev_ref, dv_ref, dvp_ref, acc
):
    head = pl.program_id(0)
    factor = SCALE * math.log2(math.e)

    @pl.when(head == 0)
    def _():
        acc[...] = jnp.zeros_like(acc)

    def tiles(full):
        for r in range(HALF // TILE):
            cols = pl.ds(r * TILE, TILE)
            q = q_ref[cols, :]
            key_place = lax.broadcasted_iota(jnp.int32, (TILE, TILE), 0)
            query_place = lax.broadcasted_iota(jnp.int32, (TILE, TILE), 1)
            scores = dot_nt(k_ref[cols, :], q)
            scores = jnp.where(key_place <= query_place, scores, -jnp.inf)
            parts = [(own_ref, r * TILE, scores)]
            sources = [(own_ref, k_ref, t) for t in range(r)]
            if full:
                sources += [(prev_ref, kp_ref, t) for t in range(HALF // TILE)]
            for place, keys, t in sources:
                parts.append((place, t * TILE, dot_nt(keys[pl.ds(t * TILE, TILE), :], q)))
            top = functools.reduce(
                jnp.maximum, [jnp.max(scores, axis=0, keepdims=True) for _, _, scores in parts]
            )
            raised = [
                (place, at, jnp.exp2((scores - top) * factor)) for place, at, scores in parts
            ]
            total = sum(jnp.sum(e, axis=0, keepdims=True) for _, _, e in raised)
            inverse = 1.0 / total
            for place, at, e in raised:
                place[0, pl.ds(at, TILE), cols] = (e * inverse).astype(BF16)

    @pl.when(flags[head] > 0)
    def _():
        tiles(True)

    @pl.when(flags[head] == 0)
    def _():
        tiles(False)

    acc[pl.ds(HALF, TILE), :] += dot_nn(own_ref[0, pl.ds(0, TILE), :], do_ref[...])
    acc[pl.ds(HALF + TILE, TILE), :] += dot_nn(
        own_ref[0, pl.ds(TILE, TILE), pl.ds(TILE, TILE)], do_ref[pl.ds(TILE, TILE), :]
    )

    @pl.when(flags[head] > 0)
    def _():
        acc[pl.ds(0, HALF), :] += dot_nn(prev_ref[0], do_ref[...])

    @pl.when(head == RATIO - 1)
    def _():
        dv_ref[...] = acc[pl.ds(HALF, HALF), :]
        dvp_ref[...] = acc[pl.ds(0, HALF), :].astype(BF16)


def score_grad_kernel(
    flags,
    own_ref,
    prev_ref,
    q_ref,
    k_ref,
    kp_ref,
    do_ref,
    v_ref,
    vp_ref,
    dq_ref,
    dk_ref,
    dkp_ref,
    acc,
    kt,
):
    head = pl.program_id(0)

    @pl.when(head == 0)
    def _():
        acc[...] = jnp.zeros_like(acc)
        kt[:, pl.ds(0, HALF)] = kp_ref[...].astype(F32).T.astype(BF16)
        kt[:, pl.ds(HALF, HALF)] = k_ref[...].astype(F32).T.astype(BF16)

    def tiles(full):
        for r in range(HALF // TILE):
            cols = pl.ds(r * TILE, TILE)
            q = q_ref[cols, :]
            do = do_ref[cols, :]
            sources = [(own_ref, v_ref, t * TILE, HALF) for t in range(r + 1)]
            if full:
                sources += [(prev_ref, vp_ref, t * TILE, 0) for t in range(HALF // TILE)]
            parts = []
            for place, values, at, base in sources:
                p = place[0, pl.ds(at, TILE), cols].astype(F32)
                parts.append((p, dot_nt(values[pl.ds(at, TILE), :], do), at + base))
            delta = sum(jnp.sum(p * d, axis=0, keepdims=True) for p, d, _ in parts)
            dq = jnp.zeros((HEAD, TILE), F32)
            for p, d, at in parts:
                score_grad = (p * (d - delta)).astype(BF16)
                dq = dq + dot_nn(kt[:, pl.ds(at, TILE)], score_grad)
                acc[pl.ds(at, TILE), :] += dot_nn(score_grad, q)
            dq_ref[cols, :] = (dq * SCALE).T.astype(BF16)

    @pl.when(flags[head] > 0)
    def _():
        tiles(True)

    @pl.when(flags[head] == 0)
    def _():
        tiles(False)

    @pl.when(head == RATIO - 1)
    def _():
        dk_ref[...] = acc[pl.ds(HALF, HALF), :] * SCALE
        dkp_ref[...] = (acc[pl.ds(0, HALF), :] * SCALE).astype(BF16)


def pack_kernel(q_ref, do_ref, k_ref, kb_ref, out_ref):
    wide = RATIO * HEAD
    out_ref[0, :, pl.ds(0, wide)] = q_ref[0, 0]
    out_ref[0, :, pl.ds(wide, wide)] = do_ref[0, 0]
    out_ref[0, :, pl.ds(2 * wide, HEAD)] = k_ref[0, 0]
    out_ref[0, :, pl.ds(2 * wide + HEAD, HEAD)] = kb_ref[0, 0]


def unpack_kernel(in_ref, dq_ref, dk_ref, sums_ref):
    wide = RATIO * HEAD
    dq_ref[0, 0] = in_ref[0, :, pl.ds(0, wide)]
    dk_ref[0, 0] = in_ref[0, :, pl.ds(wide, HEAD)]
    high = in_ref[0, :, pl.ds(wide + HEAD, HEAD)].astype(F32)
    sums_ref[...] = high + in_ref[0, :, pl.ds(wide + 2 * HEAD, HEAD)].astype(F32)


def values_kernel(odd, x_ref, mine_ref, other_ref, down_ref, up_ref, out_ref):
    up = up_ref[...].astype(F32)
    half = SHARD // 2
    for s in range(2):
        low = dot_nn(x_ref[:, pl.ds(s * SHARD, SHARD)], down_ref[...])
        values = ADAPTER_SCALE * lax.dot_general(
            low,
            up,
            (((1,), (0,)), ((), ())),
            preferred_element_type=F32,
            precision=lax.Precision.HIGHEST,
        )
        for part, first in ((mine_ref, odd[0]), (other_ref, 1 - odd[0])):
            columns = pl.ds(pl.multiple_of(s * SHARD + first * half, half), half)
            values = values + dot_nn(x_ref[:, columns], part[...])
        values = values.astype(BF16)
        for g in range(KV):
            for c in range(UNITS):
                out_ref[s * KV + g, :, pl.ds((1 + c) * HEAD, HEAD)] = values[
                    c * ROWS : (c + 1) * ROWS, g * HEAD : (g + 1) * HEAD
                ]


def merge_kernel(parts_ref, own_ref, next_ref, out_ref):
    del parts_ref
    for c in range(UNITS):
        rows = pl.ds(c * ROWS, ROWS)
        out_ref[c] = (own_ref[rows, :] + next_ref[rows, :].astype(F32)).astype(BF16)


def values_sum_kernel(parts_ref, out_ref):
    for c in range(UNITS):
        total = jnp.zeros((ROWS, HEAD), F32)
        for j in range(UNITS):
            total = total + parts_ref[j, :, pl.ds((1 + c) * HEAD, HEAD)].astype(F32)
        out_ref[pl.ds(c * ROWS, ROWS), :] = total.astype(BF16)


def adapter_kernel(dv_ref, x_ref, low_ref, up_ref, out_ref):
    width = x_ref.shape[1]
    part = x_ref.shape[0] // 2
    down = jnp.zeros((RANK, width), F32)
    for s in range(2):
        pulled = jnp.zeros((RANK, part), F32)
        for g in range(KV):
            pulled = pulled + dot_nt(up_ref[:, pl.ds(g * HEAD, HEAD)], dv_ref[s * KV + g])
        down = down + dot_nn(pulled.astype(BF16), x_ref[pl.ds(s * part, part), :])
    pieces = [down[:, c * HEAD : (c + 1) * HEAD] for c in range(width // HEAD)]
    for g in range(KV):
        up = jnp.zeros((RANK, HEAD), F32)
        for s in range(2):
            up = up + lax.dot_general(
                low_ref[s],
                dv_ref[s * KV + g].astype(F32),
                (((1,), (0,)), ((), ())),
                preferred_element_type=F32,
                precision=lax.Precision.HIGHEST,
            )
        pieces.append(up)
    out_ref[...] = jnp.zeros_like(out_ref)
    for c, piece in enumerate(pieces):
        spot = (c % PLANES) * UNITS + c // PLANES
        out_ref[pl.ds(spot * RANK, RANK), :] = piece


def call(kernel, flops, nbytes, **keywords):
    return pl.pallas_call(
        kernel,
        compiler_params=pltpu.CompilerParams(vmem_limit_bytes=VMEM),
        cost_estimate=pl.CostEstimate(flops=flops, bytes_accessed=nbytes, transcendentals=0),
        **keywords,
    )


def body(x, queries, keys, frozen, down_weight, up_weight, grads, mask):
    seq_devices = lax.axis_size("seq")
    weight_devices = lax.axis_size("wt")
    devices = seq_devices * weight_devices
    sequences, _, rows, width = x.shape
    tokens = sequences * rows
    y_planes = PLANES
    both = ("seq", "wt")
    groups = [[UNITS * y + j for j in range(UNITS)] for y in range(y_planes)]
    smem = pl.BlockSpec(memory_space=pltpu.SMEM)

    def flat(y, j, w):
        return (y * UNITS + j) * weight_devices + w

    everywhere = [
        (y, j, w) for y in range(y_planes) for j in range(UNITS) for w in range(weight_devices)
    ]
    from_before = [
        (
            flat(y, j, w),
            flat(y + 1, j, w) if y + 1 < y_planes else flat(0, j, (w + 1) % weight_devices),
        )
        for y, j, w in everywhere
    ]
    to_before = [(b, a) for a, b in from_before]
    turned = [(flat(y, w, j), flat(y, j, w)) for y, j, w in everywhere]
    next_plane = [(i, i ^ UNITS) for i in range(seq_devices)]
    same_unit = [
        [flat(y, j, w) for y in range(PLANES) for w in range(weight_devices)] for j in range(UNITS)
    ]

    def swap(block):
        return lax.all_to_all(
            block, "seq", split_axis=0, concat_axis=0, axis_index_groups=groups, tiled=True
        )

    place = lax.axis_index("seq")
    parity = (place // UNITS) % 2
    kv_head = place % KV
    my_mask = lax.dynamic_slice_in_dim(mask, kv_head * RATIO, RATIO, 0)
    flags = jnp.where(parity == 1, 1 - my_mask, my_mask).astype(jnp.int32)

    x_rows = x.reshape(tokens, width)
    wide = RATIO * HEAD

    low = jnp.dot(x_rows, down_weight, preferred_element_type=F32)
    low_parts = jnp.transpose(low.reshape(sequences, rows, RANK), (0, 2, 1))

    piece = lax.dynamic_slice_in_dim(frozen, parity * (SHARD // 2), SHARD // 2, 0)
    piece = lax.ppermute(piece, both, turned)
    keys_before = lax.ppermute(keys, both, from_before)
    token_wide = pl.BlockSpec((1, 1, rows, wide), lambda i: (i // KV, 0, 0, i % KV))
    token_head = pl.BlockSpec((1, 1, rows, HEAD), lambda i: (i // KV, 0, 0, i % KV))
    packed = 2 * (wide + HEAD)
    outgoing = call(
        pack_kernel,
        0,
        5 << 20,
        grid=(UNITS,),
        in_specs=[token_wide, token_wide, token_head, token_head],
        out_specs=pl.BlockSpec((1, rows, packed), lambda i: (i, 0, 0)),
        out_shape=pltpu.HBM((UNITS, rows, packed), BF16),
        name="pack",
    )(queries, grads, keys, keys_before)
    outgoing, piece = lax.optimization_barrier((outgoing, piece))
    first = swap(outgoing).reshape(HALF, packed)
    piece_other = lax.ppermute(piece, "seq", next_plane)
    down_part = lax.dynamic_slice_in_dim(down_weight, place % UNITS * SHARD, SHARD, 0)
    first, piece_other = lax.optimization_barrier((first, piece_other))
    features = jnp.transpose(x.reshape(sequences, rows, UNITS, SHARD), (2, 1, 0, 3))
    features = features.reshape(UNITS, rows, sequences * SHARD)
    features, first = lax.optimization_barrier((features, first))
    x_parts = swap(features).reshape(HALF, sequences * SHARD)

    head_block = pl.BlockSpec((HALF, HEAD), lambda h: (0, h))
    grad_block = pl.BlockSpec((HALF, HEAD), lambda h: (0, RATIO + h))
    key_block = pl.BlockSpec((HALF, HEAD), lambda h: (0, 2 * RATIO))
    key_prev_block = pl.BlockSpec((HALF, HEAD), lambda h: (0, 2 * RATIO + 1))
    prev_block = pl.BlockSpec((HALF, HEAD), lambda h: (0, 0))
    p_block = pl.BlockSpec((1, HALF, HALF), lambda h: (h, 0, 0))
    p_shape = pltpu.HBM((RATIO, HALF, HALF), BF16)

    product = 2 * RATIO * HALF * HALF * 3 // 2 * HEAD

    def whole(*shape):
        return pl.BlockSpec(shape, lambda i: (0,) * len(shape))

    x_block = whole(tokens, width)
    prev_one = whole(HALF, HEAD)
    weights_own, weights_prev, dv_own, dv_prev = call(
        weights_kernel,
        2 * product,
        10 << 20,
        grid=(RATIO,),
        in_specs=[smem, head_block, key_block, key_prev_block, grad_block],
        out_specs=(p_block, p_block, prev_block, prev_block),
        out_shape=(p_shape, p_shape, pltpu.HBM((HALF, HEAD), F32), pltpu.HBM((HALF, HEAD), BF16)),
        scratch_shapes=[pltpu.VMEM((2 * HALF, HEAD), F32)],
        name="weights",
    )(flags, first, first, first, first)
    weights_own = pltpu.with_memory_space_constraint(weights_own, pltpu.HBM)
    weights_prev = pltpu.with_memory_space_constraint(weights_prev, pltpu.HBM)

    dv_next = lax.ppermute(dv_prev, both, to_before)
    parts_shape = pltpu.HBM((UNITS, rows, (1 + UNITS) * HEAD), BF16)
    parts = call(
        values_kernel,
        2 * tokens * width * KV * HEAD,
        4 << 20,
        grid=(1,),
        in_specs=[
            smem,
            whole(HALF, sequences * SHARD),
            whole(SHARD // 2, KV * HEAD),
            whole(SHARD // 2, KV * HEAD),
            whole(SHARD, RANK),
            whole(RANK, KV * HEAD),
        ],
        out_specs=whole(UNITS, rows, (1 + UNITS) * HEAD),
        out_shape=parts_shape,
        name="values",
    )(parity.astype(jnp.int32).reshape(1), x_parts, piece, piece_other, down_part, up_weight)
    merged = call(
        merge_kernel,
        0,
        1 << 19,
        grid=(1,),
        in_specs=[pl.BlockSpec(memory_space=pl.ANY), prev_one, prev_one],
        out_specs=whole(UNITS, rows, HEAD),
        out_shape=parts_shape,
        input_output_aliases={0: 0},
        name="merge",
    )(parts, dv_own, dv_next)
    third = swap(merged)
    v_unit = call(
        values_sum_kernel,
        1 << 20,
        1 << 20,
        grid=(1,),
        in_specs=[whole(UNITS, rows, (1 + UNITS) * HEAD)],
        out_specs=whole(HALF, HEAD),
        out_shape=pltpu.HBM((HALF, HEAD), BF16),
        name="values_sum",
    )(third)
    v_prev = lax.ppermute(v_unit, both, from_before)

    pieces = width // HEAD + KV
    sums = call(
        adapter_kernel,
        4 * tokens * width * RANK,
        3 << 20,
        grid=(1,),
        in_specs=[
            whole(UNITS, rows, HEAD),
            x_block,
            whole(sequences, RANK, rows),
            whole(RANK, KV * HEAD),
        ],
        out_specs=whole(devices, HEAD),
        out_shape=pltpu.HBM((devices, HEAD), F32),
        name="adapter",
    )(third, x_rows, low_parts, up_weight)
    sums, v_prev = lax.optimization_barrier((sums, v_prev))
    scattered = lax.all_to_all(sums, both, split_axis=0, concat_axis=0, tiled=True)
    mine = jnp.sum(scattered, axis=0) * (ADAPTER_SCALE / math.sqrt(tokens * devices))
    peers = PLANES * weight_devices
    gathered = lax.all_to_all(
        jnp.broadcast_to(mine[None], (peers, HEAD)),
        both,
        split_axis=0,
        concat_axis=0,
        axis_index_groups=same_unit,
        tiled=True,
    )
    high = gathered.astype(BF16)
    rest = (gathered - high.astype(F32)).astype(BF16)

    dq_unit, dk_own, dk_prev = call(
        score_grad_kernel,
        3 * product,
        12 << 20,
        grid=(RATIO,),
        in_specs=[
            smem,
            p_block,
            p_block,
            head_block,
            key_block,
            key_prev_block,
            grad_block,
            prev_block,
            prev_block,
        ],
        out_specs=(head_block, prev_block, prev_block),
        out_shape=(
            pltpu.HBM((HALF, wide), BF16),
            pltpu.HBM((HALF, HEAD), F32),
            pltpu.HBM((HALF, HEAD), BF16),
        ),
        scratch_shapes=[pltpu.VMEM((2 * HALF, HEAD), F32), pltpu.VMEM((HEAD, 2 * HALF), BF16)],
        name="score_grad",
    )(
        flags,
        weights_own,
        weights_prev,
        first,
        first,
        first,
        first,
        v_unit,
        v_prev,
    )
    dk_next = lax.ppermute(dk_prev, both, to_before)
    dk_unit = (dk_own + dk_next.astype(F32)).astype(BF16)

    returning = jnp.concatenate(
        [
            dq_unit.reshape(UNITS, rows, wide),
            dk_unit.reshape(UNITS, rows, HEAD),
            jnp.broadcast_to(high[None], (UNITS, peers, HEAD)),
            jnp.broadcast_to(rest[None], (UNITS, peers, HEAD)),
        ],
        axis=2,
    )
    returned = swap(returning)

    query_grad, key_grad, totals = call(
        unpack_kernel,
        0,
        4 << 20,
        grid=(UNITS,),
        in_specs=[pl.BlockSpec((1, rows, wide + 3 * HEAD), lambda i: (i, 0, 0))],
        out_specs=(token_wide, token_head, pl.BlockSpec((peers, HEAD), lambda i: (i, 0))),
        out_shape=(
            jax.ShapeDtypeStruct((sequences, 1, rows, KV * wide), BF16),
            jax.ShapeDtypeStruct((sequences, 1, rows, KV * HEAD), BF16),
            jax.ShapeDtypeStruct((devices, HEAD), F32),
        ),
        name="unpack",
    )(returned)
    totals = totals.reshape(devices // RANK, RANK, HEAD)[:pieces]
    down_grad = jnp.transpose(totals[: width // HEAD], (0, 2, 1)).reshape(width, RANK)
    up_grad = jnp.transpose(totals[width // HEAD :], (1, 0, 2)).reshape(RANK, KV * HEAD)
    return (query_grad, key_grad, down_grad, up_grad)


def solution(mesh):
    tokens = P(None, "wt", "seq", None)
    return jax.shard_map(
        body,
        mesh=mesh,
        in_specs=(tokens, tokens, tokens, P("wt", None), P(), P(), tokens, P()),
        out_specs=(tokens, tokens, P(), P()),
        check_vma=False,
    )
```

```python
import functools
import math

import jax
import jax.numpy as jnp
from jax import lax
from jax.experimental import pallas as pl
from jax.experimental.pallas import tpu as pltpu
from jax.sharding import PartitionSpec as P

HEAD = 128
HALF = 512
TILE = 256
RATIO = 8
KV = 4
RANK = 8
UNITS = 8
PLANES = 8
SHARD = 512
ROWS = 64
BATCH = 2
SCALE = 1.0 / math.sqrt(HEAD)
ADAPTER_SCALE = 2.0
VMEM = 48 * 1024 * 1024
F32 = jnp.float32
BF16 = jnp.bfloat16


def dot_nt(a, b):
    return lax.dot_general(a, b, (((1,), (1,)), ((), ())), preferred_element_type=F32)


def dot_nn(a, b):
    return lax.dot_general(a, b, (((1,), (0,)), ((), ())), preferred_element_type=F32)


def weights_kernel(
    flags, q_ref, k_ref, kp_ref, do_ref, own_ref, prev_ref, dv_ref, dvp_ref, acc
):
    step = pl.program_id(0)
    factor = SCALE * math.log2(math.e)

    @pl.when(step == 0)
    def _():
        acc[...] = jnp.zeros_like(acc)

    def tiles(i, full):
        head = pl.ds(i * HEAD, HEAD)
        for r in range(HALF // TILE):
            cols = pl.ds(r * TILE, TILE)
            q = q_ref[cols, head]
            key_place = lax.broadcasted_iota(jnp.int32, (TILE, TILE), 0)
            query_place = lax.broadcasted_iota(jnp.int32, (TILE, TILE), 1)
            scores = dot_nt(k_ref[cols, :], q)
            scores = jnp.where(key_place <= query_place, scores, -jnp.inf)
            parts = [(own_ref, r * TILE, scores)]
            sources = [(own_ref, k_ref, t) for t in range(r)]
            if full:
                sources += [(prev_ref, kp_ref, t) for t in range(HALF // TILE)]
            for place, keys, t in sources:
                parts.append((place, t * TILE, dot_nt(keys[pl.ds(t * TILE, TILE), :], q)))
            top = functools.reduce(
                jnp.maximum, [jnp.max(scores, axis=0, keepdims=True) for _, _, scores in parts]
            )
            raised = [
                (place, at, jnp.exp2((scores - top) * factor)) for place, at, scores in parts
            ]
            total = sum(jnp.sum(e, axis=0, keepdims=True) for _, _, e in raised)
            inverse = 1.0 / total
            for place, at, e in raised:
                place[i, pl.ds(at, TILE), cols] = (e * inverse).astype(BF16)
        do = do_ref[:, head]
        acc[pl.ds(HALF, TILE), :] += dot_nn(own_ref[i, pl.ds(0, TILE), :], do)
        acc[pl.ds(HALF + TILE, TILE), :] += dot_nn(
            own_ref[i, pl.ds(TILE, TILE), pl.ds(TILE, TILE)], do[TILE:]
        )
        if full:
            acc[pl.ds(0, HALF), :] += dot_nn(prev_ref[i], do)

    for i in range(BATCH):

        @pl.when(flags[step * BATCH + i] > 0)
        def _(i=i):
            tiles(i, True)

        @pl.when(flags[step * BATCH + i] == 0)
        def _(i=i):
            tiles(i, False)

    @pl.when(step == RATIO // BATCH - 1)
    def _():
        dv_ref[...] = acc[pl.ds(HALF, HALF), :]
        dvp_ref[...] = acc[pl.ds(0, HALF), :].astype(BF16)


def score_grad_kernel(
    flags,
    own_ref,
    prev_ref,
    q_ref,
    k_ref,
    kp_ref,
    do_ref,
    v_ref,
    vp_ref,
    dq_ref,
    dk_ref,
    dkp_ref,
    acc,
    kt,
):
    step = pl.program_id(0)

    @pl.when(step == 0)
    def _():
        acc[...] = jnp.zeros_like(acc)
        kt[:, pl.ds(0, HALF)] = kp_ref[...].astype(F32).T.astype(BF16)
        kt[:, pl.ds(HALF, HALF)] = k_ref[...].astype(F32).T.astype(BF16)

    def tiles(i, full):
        head = pl.ds(i * HEAD, HEAD)
        for r in range(HALF // TILE):
            cols = pl.ds(r * TILE, TILE)
            q = q_ref[cols, head]
            do = do_ref[cols, head]
            sources = [(own_ref, v_ref, t * TILE, HALF) for t in range(r + 1)]
            if full:
                sources += [(prev_ref, vp_ref, t * TILE, 0) for t in range(HALF // TILE)]
            parts = []
            for place, values, at, base in sources:
                p = place[i, pl.ds(at, TILE), cols].astype(F32)
                parts.append((p, dot_nt(values[pl.ds(at, TILE), :], do), at + base))
            delta = sum(jnp.sum(p * d, axis=0, keepdims=True) for p, d, _ in parts)
            dq = jnp.zeros((HEAD, TILE), F32)
            for p, d, at in parts:
                score_grad = (p * (d - delta)).astype(BF16)
                dq = dq + dot_nn(kt[:, pl.ds(at, TILE)], score_grad)
                acc[pl.ds(at, TILE), :] += dot_nn(score_grad, q)
            dq_ref[cols, head] = (dq * SCALE).T.astype(BF16)

    for i in range(BATCH):

        @pl.when(flags[step * BATCH + i] > 0)
        def _(i=i):
            tiles(i, True)

        @pl.when(flags[step * BATCH + i] == 0)
        def _(i=i):
            tiles(i, False)

    @pl.when(step == RATIO // BATCH - 1)
    def _():
        dk_ref[...] = (acc[pl.ds(HALF, HALF), :] * SCALE).astype(BF16)
        dkp_ref[...] = (acc[pl.ds(0, HALF), :] * SCALE).astype(BF16)


def features_kernel(x_ref, out_ref):
    for j in range(UNITS):
        for s in range(2):
            out_ref[j, :, pl.ds(s * SHARD, SHARD)] = x_ref[s, 0, :, pl.ds(j * SHARD, SHARD)]


def pack_kernel(q_ref, do_ref, out_ref):
    wide = RATIO * HEAD
    for g in range(KV):
        heads = pl.ds(g * wide, wide)
        out_ref[g, :, pl.ds(0, wide)] = q_ref[0, 0, :, heads]
        out_ref[g, :, pl.ds(wide, wide)] = do_ref[0, 0, :, heads]


def pack_keys_kernel(packed_ref, k_ref, kb_ref, out_ref):
    del packed_ref
    for s in range(2):
        for g in range(KV):
            heads = pl.ds(g * HEAD, HEAD)
            out_ref[s * KV + g, :, pl.ds(0, HEAD)] = k_ref[s, 0, :, heads]
            out_ref[s * KV + g, :, pl.ds(HEAD, HEAD)] = kb_ref[s, 0, :, heads]


def unpack_kernel(in_ref, dq_ref, dk_ref):
    wide = RATIO * HEAD
    for g in range(KV):
        dq_ref[0, 0, :, pl.ds(g * wide, wide)] = in_ref[g, :, pl.ds(0, wide)]
        dk_ref[0, 0, :, pl.ds(g * HEAD, HEAD)] = in_ref[g, :, pl.ds(wide, HEAD)]


def split_float(x):
    high = x.astype(BF16)
    return high, (x - high.astype(F32)).astype(BF16)


def values_kernel(odd, x_ref, mine_ref, other_ref, down_ref, up_ref, out_ref):
    half = SHARD // 2
    high, rest = split_float(ADAPTER_SCALE * dot_nn(x_ref[...], down_ref[...]))
    values = dot_nn(high, up_ref[...]) + dot_nn(rest, up_ref[...])
    for part, first in ((mine_ref, odd[0]), (other_ref, 1 - odd[0])):
        columns = pl.ds(pl.multiple_of(first * half, half), half)
        values = values + dot_nn(x_ref[:, columns], part[...])
    values = values.astype(BF16)
    for g in range(KV):
        for c in range(UNITS):
            out_ref[g, :, pl.ds((1 + c) * HEAD, HEAD)] = values[
                c * ROWS : (c + 1) * ROWS, g * HEAD : (g + 1) * HEAD
            ]


def merge_kernel(parts_ref, own_ref, next_ref, out_ref):
    del parts_ref
    for c in range(UNITS):
        rows = pl.ds(c * ROWS, ROWS)
        out_ref[c] = (own_ref[rows, :] + next_ref[rows, :].astype(F32)).astype(BF16)


def values_sum_kernel(parts_ref, out_ref):
    for c in range(UNITS):
        total = jnp.zeros((ROWS, HEAD), F32)
        for j in range(UNITS):
            total = total + parts_ref[j, :, pl.ds((1 + c) * HEAD, HEAD)].astype(F32)
        out_ref[pl.ds(c * ROWS, ROWS), :] = total.astype(BF16)


def adapter_kernel(dv_ref, x_ref, low_ref, up_ref, out_ref):
    width = x_ref.shape[1]
    part = x_ref.shape[0] // 2
    down = jnp.zeros((RANK, width), F32)
    for s in range(2):
        pulled = jnp.zeros((RANK, part), F32)
        for g in range(KV):
            pulled = pulled + dot_nt(up_ref[:, pl.ds(g * HEAD, HEAD)], dv_ref[s * KV + g])
        down = down + dot_nn(pulled.astype(BF16), x_ref[pl.ds(s * part, part), :])
    pieces = [down[:, c * HEAD : (c + 1) * HEAD] for c in range(width // HEAD)]
    lows = [split_float(low_ref[s]) for s in range(2)]
    for g in range(KV):
        up = jnp.zeros((RANK, HEAD), F32)
        for s in range(2):
            for low in lows[s]:
                up = up + dot_nn(low, dv_ref[s * KV + g])
        pieces.append(up)
    for c, piece in enumerate(pieces):
        out_ref[pl.ds(c * RANK, RANK), :] = piece
    used = len(pieces) * RANK
    out_ref[pl.ds(used, out_ref.shape[0] - used), :] = jnp.zeros(
        (out_ref.shape[0] - used, HEAD), F32
    )


def call(kernel, flops, nbytes, **keywords):
    return pl.pallas_call(
        kernel,
        compiler_params=pltpu.CompilerParams(vmem_limit_bytes=VMEM),
        cost_estimate=pl.CostEstimate(flops=flops, bytes_accessed=nbytes, transcendentals=0),
        **keywords,
    )


def body(x, queries, keys, frozen, down_weight, up_weight, grads, mask):
    seq_devices = lax.axis_size("seq")
    weight_devices = lax.axis_size("wt")
    devices = seq_devices * weight_devices
    sequences, _, rows, width = x.shape
    tokens = sequences * rows
    y_planes = PLANES
    both = ("seq", "wt")
    groups = [[UNITS * y + j for j in range(UNITS)] for y in range(y_planes)]
    smem = pl.BlockSpec(memory_space=pltpu.SMEM)

    def flat(y, j, w):
        return (y * UNITS + j) * weight_devices + w

    everywhere = [
        (y, j, w) for y in range(y_planes) for j in range(UNITS) for w in range(weight_devices)
    ]
    from_before = [
        (
            flat(y, j, w),
            flat(y + 1, j, w) if y + 1 < y_planes else flat(0, j, (w + 1) % weight_devices),
        )
        for y, j, w in everywhere
    ]
    to_before = [(b, a) for a, b in from_before]
    turned = [(flat(y, w, j), flat(y, j, w)) for y, j, w in everywhere]
    next_plane = [(i, i ^ UNITS) for i in range(seq_devices)]
    same_unit = [
        [flat(y, j, w) for y in range(PLANES) for w in range(weight_devices)] for j in range(UNITS)
    ]

    def swap(block):
        return lax.all_to_all(
            block, "seq", split_axis=0, concat_axis=0, axis_index_groups=groups, tiled=True
        )

    place = lax.axis_index("seq")
    parity = (place // UNITS) % 2
    kv_head = place % KV
    my_mask = lax.dynamic_slice_in_dim(mask, kv_head * RATIO, RATIO, 0)
    flags = jnp.where(parity == 1, 1 - my_mask, my_mask).astype(jnp.int32)

    x_rows = x.reshape(tokens, width)
    wide = RATIO * HEAD

    low = jnp.dot(x_rows, down_weight, preferred_element_type=F32)
    low_parts = jnp.transpose(low.reshape(sequences, rows, RANK), (0, 2, 1))

    def whole(*shape):
        return pl.BlockSpec(shape, lambda i: (0,) * len(shape))

    features = call(
        features_kernel,
        0,
        2 << 20,
        grid=(1,),
        in_specs=[whole(sequences, 1, rows, width)],
        out_specs=whole(UNITS, rows, sequences * SHARD),
        out_shape=pltpu.HBM((UNITS, rows, sequences * SHARD), BF16),
        name="features",
    )(pltpu.with_memory_space_constraint(x, pltpu.HBM))
    x_parts = swap(features).reshape(HALF, sequences * SHARD)
    piece = lax.dynamic_slice_in_dim(frozen, parity * (SHARD // 2), SHARD // 2, 0)
    piece = lax.ppermute(piece, both, turned)
    keys_before = lax.ppermute(keys, both, from_before)
    token_wide = pl.BlockSpec((1, 1, rows, KV * wide), lambda i: (i, 0, 0, 0))
    token_head = pl.BlockSpec((1, 1, rows, KV * HEAD), lambda i: (i, 0, 0, 0))
    packed = 2 * (wide + HEAD)
    packed_shape = pltpu.HBM((UNITS, rows, packed), BF16)
    outgoing = call(
        pack_kernel,
        0,
        4 << 20,
        grid=(sequences,),
        in_specs=[token_wide, token_wide],
        out_specs=pl.BlockSpec((KV, rows, 2 * wide), lambda i: (i, 0, 0)),
        out_shape=packed_shape,
        name="pack",
    )(
        pltpu.with_memory_space_constraint(queries, pltpu.HBM),
        pltpu.with_memory_space_constraint(grads, pltpu.HBM),
    )
    all_keys = whole(sequences, 1, rows, KV * HEAD)
    outgoing = call(
        pack_keys_kernel,
        0,
        1 << 19,
        grid=(1,),
        in_specs=[pl.BlockSpec(memory_space=pl.ANY), all_keys, all_keys],
        out_specs=pl.BlockSpec((UNITS, rows, 2 * HEAD), lambda i: (0, 0, RATIO)),
        out_shape=packed_shape,
        input_output_aliases={0: 0},
        name="pack_keys",
    )(outgoing, keys, keys_before)
    outgoing, piece, x_parts = lax.optimization_barrier((outgoing, piece, x_parts))
    first = swap(outgoing).reshape(HALF, packed)
    piece_other = lax.ppermute(piece, "seq", next_plane)
    down_part = lax.dynamic_slice_in_dim(down_weight, place % UNITS * SHARD, SHARD, 0)
    first, piece_other, down_part, low_parts = lax.optimization_barrier(
        (first, piece_other, down_part, low_parts)
    )

    steps = RATIO // BATCH
    head_block = pl.BlockSpec((HALF, BATCH * HEAD), lambda h: (0, h))
    grad_block = pl.BlockSpec((HALF, BATCH * HEAD), lambda h: (0, steps + h))
    key_block = pl.BlockSpec((HALF, HEAD), lambda h: (0, 2 * RATIO))
    key_prev_block = pl.BlockSpec((HALF, HEAD), lambda h: (0, 2 * RATIO + 1))
    prev_block = pl.BlockSpec((HALF, HEAD), lambda h: (0, 0))
    p_block = pl.BlockSpec((BATCH, HALF, HALF), lambda h: (h, 0, 0))
    p_shape = pltpu.HBM((RATIO, HALF, HALF), BF16)

    product = 2 * RATIO * HALF * HALF * 3 // 2 * HEAD

    x_block = whole(tokens, width)
    prev_one = whole(HALF, HEAD)
    weights_own, weights_prev, dv_own, dv_prev = call(
        weights_kernel,
        2 * product,
        10 << 20,
        grid=(steps,),
        in_specs=[smem, head_block, key_block, key_prev_block, grad_block],
        out_specs=(p_block, p_block, prev_block, prev_block),
        out_shape=(p_shape, p_shape, pltpu.HBM((HALF, HEAD), F32), pltpu.HBM((HALF, HEAD), BF16)),
        scratch_shapes=[pltpu.VMEM((2 * HALF, HEAD), F32)],
        name="weights",
    )(flags, first, first, first, first)
    weights_own = pltpu.with_memory_space_constraint(weights_own, pltpu.HBM)
    weights_prev = pltpu.with_memory_space_constraint(weights_prev, pltpu.HBM)

    dv_next = lax.ppermute(dv_prev, both, to_before)
    parts_shape = pltpu.HBM((UNITS, rows, (1 + UNITS) * HEAD), BF16)
    parts = call(
        values_kernel,
        2 * tokens * width * KV * HEAD,
        4 << 20,
        grid=(sequences,),
        in_specs=[
            smem,
            pl.BlockSpec((HALF, SHARD), lambda i: (0, i)),
            whole(SHARD // 2, KV * HEAD),
            whole(SHARD // 2, KV * HEAD),
            whole(SHARD, RANK),
            whole(RANK, KV * HEAD),
        ],
        out_specs=pl.BlockSpec((KV, rows, (1 + UNITS) * HEAD), lambda i: (i, 0, 0)),
        out_shape=parts_shape,
        name="values",
    )(parity.astype(jnp.int32).reshape(1), x_parts, piece, piece_other, down_part, up_weight)
    merged = call(
        merge_kernel,
        0,
        1 << 19,
        grid=(1,),
        in_specs=[pl.BlockSpec(memory_space=pl.ANY), prev_one, prev_one],
        out_specs=whole(UNITS, rows, HEAD),
        out_shape=parts_shape,
        input_output_aliases={0: 0},
        name="merge",
    )(parts, dv_own, dv_next)
    third = swap(merged)
    v_unit = call(
        values_sum_kernel,
        1 << 20,
        1 << 20,
        grid=(1,),
        in_specs=[whole(UNITS, rows, (1 + UNITS) * HEAD)],
        out_specs=whole(HALF, HEAD),
        out_shape=pltpu.HBM((HALF, HEAD), BF16),
        name="values_sum",
    )(third)
    v_prev = lax.ppermute(v_unit, both, from_before)

    pieces = width // HEAD + KV
    peers = PLANES * weight_devices
    share = RANK
    sums = call(
        adapter_kernel,
        4 * tokens * width * RANK,
        3 << 20,
        grid=(1,),
        in_specs=[
            whole(UNITS, rows, HEAD),
            x_block,
            whole(sequences, RANK, rows),
            whole(RANK, KV * HEAD),
        ],
        out_specs=whole(peers * share, HEAD),
        out_shape=pltpu.HBM((peers * share, HEAD), F32),
        name="adapter",
    )(third, x_rows, low_parts, up_weight)
    v_prev, sums = lax.optimization_barrier((v_prev, sums))

    def among_peers(block):
        return lax.all_to_all(
            block, both, split_axis=0, concat_axis=0, axis_index_groups=same_unit, tiled=True
        ).reshape(peers, share, HEAD)

    mine = jnp.sum(among_peers(sums), axis=0) * (ADAPTER_SCALE / math.sqrt(tokens * devices))
    blank = jnp.zeros((rows // 2 - share, HEAD), BF16)
    high, rest = split_float(mine)
    mine_parts = jnp.concatenate([high, blank, rest, blank], axis=0)

    dq_unit, dk_own, dk_prev = call(
        score_grad_kernel,
        3 * product,
        12 << 20,
        grid=(steps,),
        in_specs=[
            smem,
            p_block,
            p_block,
            head_block,
            key_block,
            key_prev_block,
            grad_block,
            prev_block,
            prev_block,
        ],
        out_specs=(head_block, prev_block, prev_block),
        out_shape=(
            pltpu.HBM((HALF, wide), BF16),
            pltpu.HBM((HALF, HEAD), BF16),
            pltpu.HBM((HALF, HEAD), BF16),
        ),
        scratch_shapes=[pltpu.VMEM((2 * HALF, HEAD), F32), pltpu.VMEM((HEAD, 2 * HALF), BF16)],
        name="score_grad",
    )(
        flags,
        weights_own,
        weights_prev,
        first,
        first,
        first,
        first,
        v_unit,
        v_prev,
    )
    returning = jnp.concatenate(
        [
            dq_unit.reshape(UNITS, rows, wide),
            dk_own.reshape(UNITS, rows, HEAD),
            dk_prev.reshape(UNITS, rows, HEAD),
            jnp.broadcast_to(mine_parts[None], (UNITS, rows, HEAD)),
        ],
        axis=2,
    )
    returned = swap(returning)

    sum_parts = returned[:, :, wide + 2 * HEAD :].reshape(UNITS * 2, rows // 2, HEAD)
    total = jnp.sum(sum_parts[:, :share].astype(F32), axis=0)
    spread = jnp.broadcast_to(total[None], (peers, share, HEAD)).reshape(peers * share, HEAD)
    key_prev = returned[:, :, wide + HEAD : wide + 2 * HEAD]
    key_prev, spread = lax.optimization_barrier((key_prev, spread))
    totals = among_peers(spread).reshape(peers * share, HEAD)[: pieces * RANK]
    totals = totals.reshape(pieces, RANK, HEAD)

    key_shape = jax.ShapeDtypeStruct((sequences, 1, rows, KV * HEAD), BF16)
    query_grad, key_own = call(
        unpack_kernel,
        0,
        4 << 20,
        grid=(sequences,),
        in_specs=[pl.BlockSpec((KV, rows, wide + HEAD), lambda i: (i, 0, 0))],
        out_specs=(token_wide, token_head),
        out_shape=(
            jax.ShapeDtypeStruct((sequences, 1, rows, KV * wide), BF16),
            jax.ShapeDtypeStruct((sequences, 1, rows, KV * HEAD), BF16),
        ),
        name="unpack",
    )(returned)
    key_next = lax.ppermute(key_prev, both, to_before)
    key_next = jnp.transpose(key_next.reshape(sequences, KV, rows, HEAD), (0, 2, 1, 3))
    key_next = key_next.reshape(sequences, 1, rows, KV * HEAD)
    key_grad = (key_own.astype(F32) + key_next.astype(F32)).astype(BF16)
    down_grad = jnp.transpose(totals[: width // HEAD], (0, 2, 1)).reshape(width, RANK)
    up_grad = jnp.transpose(totals[width // HEAD :], (1, 0, 2)).reshape(RANK, KV * HEAD)
    return (query_grad, key_grad, down_grad, up_grad)


def solution(mesh):
    tokens = P(None, "wt", "seq", None)
    return jax.shard_map(
        body,
        mesh=mesh,
        in_specs=(tokens, tokens, tokens, P("wt", None), P(), P(), tokens, P()),
        out_specs=(tokens, tokens, P(), P()),
        check_vma=False,
    )
```

```python
import functools
import math

import jax
import jax.numpy as jnp
from jax import lax
from jax.experimental import pallas as pl
from jax.experimental.pallas import tpu as pltpu
from jax.sharding import PartitionSpec as P

HEAD = 128
HALF = 512
TILE = 256
RATIO = 8
KV = 4
RANK = 8
UNITS = 8
PLANES = 8
SHARD = 512
ROWS = 64
BATCH = 2
SCALE = 1.0 / math.sqrt(HEAD)
ADAPTER_SCALE = 2.0
VMEM = 48 * 1024 * 1024
F32 = jnp.float32
BF16 = jnp.bfloat16


def dot_nt(a, b):
    return lax.dot_general(a, b, (((1,), (1,)), ((), ())), preferred_element_type=F32)


def dot_nn(a, b):
    return lax.dot_general(a, b, (((1,), (0,)), ((), ())), preferred_element_type=F32)


def weights_kernel(
    flags, q_ref, k_ref, kp_ref, do_ref, own_ref, prev_ref, dv_ref, dvp_ref, acc
):
    step = pl.program_id(0)
    factor = SCALE * math.log2(math.e)

    @pl.when(step == 0)
    def _():
        acc[...] = jnp.zeros_like(acc)

    def tiles(i, full):
        head = pl.ds(i * HEAD, HEAD)
        for r in range(HALF // TILE):
            cols = pl.ds(r * TILE, TILE)
            q = q_ref[cols, head]
            key_place = lax.broadcasted_iota(jnp.int32, (TILE, TILE), 0)
            query_place = lax.broadcasted_iota(jnp.int32, (TILE, TILE), 1)
            scores = dot_nt(k_ref[cols, :], q)
            scores = jnp.where(key_place <= query_place, scores, -jnp.inf)
            parts = [(own_ref, r * TILE, scores)]
            sources = [(own_ref, k_ref, t) for t in range(r)]
            if full:
                sources += [(prev_ref, kp_ref, t) for t in range(HALF // TILE)]
            for place, keys, t in sources:
                parts.append((place, t * TILE, dot_nt(keys[pl.ds(t * TILE, TILE), :], q)))
            top = functools.reduce(
                jnp.maximum, [jnp.max(scores, axis=0, keepdims=True) for _, _, scores in parts]
            )
            raised = [
                (place, at, jnp.exp2((scores - top) * factor)) for place, at, scores in parts
            ]
            total = sum(jnp.sum(e, axis=0, keepdims=True) for _, _, e in raised)
            inverse = 1.0 / total
            for place, at, e in raised:
                place[i, pl.ds(at, TILE), cols] = (e * inverse).astype(BF16)
        do = do_ref[:, head]
        acc[pl.ds(HALF, TILE), :] += dot_nn(own_ref[i, pl.ds(0, TILE), :], do)
        acc[pl.ds(HALF + TILE, TILE), :] += dot_nn(
            own_ref[i, pl.ds(TILE, TILE), pl.ds(TILE, TILE)], do[TILE:]
        )
        if full:
            acc[pl.ds(0, HALF), :] += dot_nn(prev_ref[i], do)

    for i in range(BATCH):

        @pl.when(flags[step * BATCH + i] > 0)
        def _(i=i):
            tiles(i, True)

        @pl.when(flags[step * BATCH + i] == 0)
        def _(i=i):
            tiles(i, False)

    @pl.when(step == RATIO // BATCH - 1)
    def _():
        dv_ref[...] = acc[pl.ds(HALF, HALF), :]
        dvp_ref[...] = acc[pl.ds(0, HALF), :].astype(BF16)


def score_grad_kernel(
    flags,
    own_ref,
    prev_ref,
    q_ref,
    k_ref,
    kp_ref,
    do_ref,
    v_ref,
    vp_ref,
    dq_ref,
    dk_ref,
    dkp_ref,
    acc,
    kt,
):
    step = pl.program_id(0)

    @pl.when(step == 0)
    def _():
        acc[...] = jnp.zeros_like(acc)
        kt[:, pl.ds(0, HALF)] = kp_ref[...].astype(F32).T.astype(BF16)
        kt[:, pl.ds(HALF, HALF)] = k_ref[...].astype(F32).T.astype(BF16)

    def tiles(i, full):
        head = pl.ds(i * HEAD, HEAD)
        for r in range(HALF // TILE):
            cols = pl.ds(r * TILE, TILE)
            q = q_ref[cols, head]
            do = do_ref[cols, head]
            sources = [(own_ref, v_ref, t * TILE, HALF) for t in range(r + 1)]
            if full:
                sources += [(prev_ref, vp_ref, t * TILE, 0) for t in range(HALF // TILE)]
            parts = []
            for place, values, at, base in sources:
                p = place[i, pl.ds(at, TILE), cols].astype(F32)
                parts.append((p, dot_nt(values[pl.ds(at, TILE), :], do), at + base))
            delta = sum(jnp.sum(p * d, axis=0, keepdims=True) for p, d, _ in parts)
            dq = jnp.zeros((HEAD, TILE), F32)
            for p, d, at in parts:
                score_grad = (p * (d - delta)).astype(BF16)
                dq = dq + dot_nn(kt[:, pl.ds(at, TILE)], score_grad)
                acc[pl.ds(at, TILE), :] += dot_nn(score_grad, q)
            dq_ref[cols, head] = (dq * SCALE).T.astype(BF16)

    for i in range(BATCH):

        @pl.when(flags[step * BATCH + i] > 0)
        def _(i=i):
            tiles(i, True)

        @pl.when(flags[step * BATCH + i] == 0)
        def _(i=i):
            tiles(i, False)

    @pl.when(step == RATIO // BATCH - 1)
    def _():
        dk_ref[...] = (acc[pl.ds(HALF, HALF), :] * SCALE).astype(BF16)
        dkp_ref[...] = (acc[pl.ds(0, HALF), :] * SCALE).astype(BF16)


def pack_kernel(q_ref, do_ref, out_ref):
    wide = RATIO * HEAD
    for g in range(KV):
        heads = pl.ds(g * wide, wide)
        out_ref[g, :, pl.ds(0, wide)] = q_ref[0, 0, :, heads]
        out_ref[g, :, pl.ds(wide, wide)] = do_ref[0, 0, :, heads]


def pack_keys_kernel(packed_ref, k_ref, kb_ref, out_ref):
    del packed_ref
    for s in range(2):
        for g in range(KV):
            heads = pl.ds(g * HEAD, HEAD)
            out_ref[s * KV + g, :, pl.ds(0, HEAD)] = k_ref[s, 0, :, heads]
            out_ref[s * KV + g, :, pl.ds(HEAD, HEAD)] = kb_ref[s, 0, :, heads]


def unpack_kernel(in_ref, dq_ref, dk_ref):
    wide = RATIO * HEAD
    for g in range(KV):
        dq_ref[0, 0, :, pl.ds(g * wide, wide)] = in_ref[g, :, pl.ds(0, wide)]
        dk_ref[0, 0, :, pl.ds(g * HEAD, HEAD)] = in_ref[g, :, pl.ds(wide, HEAD)]


def split_float(x):
    high = x.astype(BF16)
    return high, (x - high.astype(F32)).astype(BF16)


def values_kernel(odd, x_ref, mine_ref, other_ref, down_ref, up_ref, out_ref):
    half = SHARD // 2
    high, rest = split_float(ADAPTER_SCALE * dot_nn(x_ref[...], down_ref[...]))
    values = dot_nn(high, up_ref[...]) + dot_nn(rest, up_ref[...])
    for part, first in ((mine_ref, odd[0]), (other_ref, 1 - odd[0])):
        columns = pl.ds(pl.multiple_of(first * half, half), half)
        values = values + dot_nn(x_ref[:, columns], part[...])
    values = values.astype(BF16)
    for g in range(KV):
        for c in range(UNITS):
            out_ref[g, :, pl.ds((1 + c) * HEAD, HEAD)] = values[
                c * ROWS : (c + 1) * ROWS, g * HEAD : (g + 1) * HEAD
            ]


def merge_kernel(parts_ref, own_ref, next_ref, out_ref):
    del parts_ref
    for c in range(UNITS):
        rows = pl.ds(c * ROWS, ROWS)
        out_ref[c] = (own_ref[rows, :] + next_ref[rows, :].astype(F32)).astype(BF16)


def values_sum_kernel(parts_ref, out_ref):
    for c in range(UNITS):
        total = jnp.zeros((ROWS, HEAD), F32)
        for j in range(UNITS):
            total = total + parts_ref[j, :, pl.ds((1 + c) * HEAD, HEAD)].astype(F32)
        out_ref[pl.ds(c * ROWS, ROWS), :] = total.astype(BF16)


def adapter_kernel(dv_ref, x_ref, low_ref, up_ref, out_ref):
    width = x_ref.shape[1]
    part = x_ref.shape[0] // 2
    down = jnp.zeros((RANK, width), F32)
    for s in range(2):
        pulled = jnp.zeros((RANK, part), F32)
        for g in range(KV):
            pulled = pulled + dot_nt(up_ref[:, pl.ds(g * HEAD, HEAD)], dv_ref[s * KV + g])
        down = down + dot_nn(pulled.astype(BF16), x_ref[pl.ds(s * part, part), :])
    pieces = [down[:, c * HEAD : (c + 1) * HEAD] for c in range(width // HEAD)]
    lows = [split_float(low_ref[s]) for s in range(2)]
    for g in range(KV):
        up = jnp.zeros((RANK, HEAD), F32)
        for s in range(2):
            for low in lows[s]:
                up = up + dot_nn(low, dv_ref[s * KV + g])
        pieces.append(up)
    for c, piece in enumerate(pieces):
        out_ref[pl.ds(c * RANK, RANK), :] = piece
    used = len(pieces) * RANK
    out_ref[pl.ds(used, out_ref.shape[0] - used), :] = jnp.zeros(
        (out_ref.shape[0] - used, HEAD), F32
    )


def call(kernel, flops, nbytes, **keywords):
    return pl.pallas_call(
        kernel,
        compiler_params=pltpu.CompilerParams(vmem_limit_bytes=VMEM),
        cost_estimate=pl.CostEstimate(flops=flops, bytes_accessed=nbytes, transcendentals=0),
        **keywords,
    )


def body(x, queries, keys, frozen, down_weight, up_weight, grads, mask):
    seq_devices = lax.axis_size("seq")
    weight_devices = lax.axis_size("wt")
    devices = seq_devices * weight_devices
    sequences, _, rows, width = x.shape
    tokens = sequences * rows
    y_planes = PLANES
    both = ("seq", "wt")
    groups = [[UNITS * y + j for j in range(UNITS)] for y in range(y_planes)]
    smem = pl.BlockSpec(memory_space=pltpu.SMEM)

    def flat(y, j, w):
        return (y * UNITS + j) * weight_devices + w

    everywhere = [
        (y, j, w) for y in range(y_planes) for j in range(UNITS) for w in range(weight_devices)
    ]
    from_before = [
        (
            flat(y, j, w),
            flat(y + 1, j, w) if y + 1 < y_planes else flat(0, j, (w + 1) % weight_devices),
        )
        for y, j, w in everywhere
    ]
    to_before = [(b, a) for a, b in from_before]
    turned = [(flat(y, w, j), flat(y, j, w)) for y, j, w in everywhere]
    next_plane = [(i, i ^ UNITS) for i in range(seq_devices)]
    same_unit = [
        [flat(y, j, w) for y in range(PLANES) for w in range(weight_devices)] for j in range(UNITS)
    ]

    def swap(block):
        return lax.all_to_all(
            block, "seq", split_axis=0, concat_axis=0, axis_index_groups=groups, tiled=True
        )

    place = lax.axis_index("seq")
    parity = (place // UNITS) % 2
    kv_head = place % KV
    my_mask = lax.dynamic_slice_in_dim(mask, kv_head * RATIO, RATIO, 0)
    flags = jnp.where(parity == 1, 1 - my_mask, my_mask).astype(jnp.int32)

    x_rows = x.reshape(tokens, width)
    wide = RATIO * HEAD

    low = jnp.dot(x_rows, down_weight, preferred_element_type=F32)
    low_parts = jnp.transpose(low.reshape(sequences, rows, RANK), (0, 2, 1))

    def whole(*shape):
        return pl.BlockSpec(shape, lambda i: (0,) * len(shape))

    piece = lax.dynamic_slice_in_dim(frozen, parity * (SHARD // 2), SHARD // 2, 0)
    piece = lax.ppermute(piece, both, turned)
    keys_before = lax.ppermute(keys, both, from_before)
    token_wide = pl.BlockSpec((1, 1, rows, KV * wide), lambda i: (i, 0, 0, 0))
    token_head = pl.BlockSpec((1, 1, rows, KV * HEAD), lambda i: (i, 0, 0, 0))
    packed = 2 * (wide + HEAD)
    packed_shape = pltpu.HBM((UNITS, rows, packed), BF16)
    outgoing = call(
        pack_kernel,
        0,
        4 << 20,
        grid=(sequences,),
        in_specs=[token_wide, token_wide],
        out_specs=pl.BlockSpec((KV, rows, 2 * wide), lambda i: (i, 0, 0)),
        out_shape=packed_shape,
        name="pack",
    )(
        pltpu.with_memory_space_constraint(queries, pltpu.HBM),
        pltpu.with_memory_space_constraint(grads, pltpu.HBM),
    )
    all_keys = whole(sequences, 1, rows, KV * HEAD)
    outgoing = call(
        pack_keys_kernel,
        0,
        1 << 19,
        grid=(1,),
        in_specs=[pl.BlockSpec(memory_space=pl.ANY), all_keys, all_keys],
        out_specs=pl.BlockSpec((UNITS, rows, 2 * HEAD), lambda i: (0, 0, RATIO)),
        out_shape=packed_shape,
        input_output_aliases={0: 0},
        name="pack_keys",
    )(outgoing, keys, keys_before)
    outgoing, piece = lax.optimization_barrier((outgoing, piece))
    first = swap(outgoing).reshape(HALF, packed)
    piece_other = lax.ppermute(piece, "seq", next_plane)
    down_part = lax.dynamic_slice_in_dim(down_weight, place % UNITS * SHARD, SHARD, 0)
    first, piece_other, down_part, low_parts = lax.optimization_barrier(
        (first, piece_other, down_part, low_parts)
    )
    features = jnp.transpose(x.reshape(sequences, rows, UNITS, SHARD), (2, 1, 0, 3))
    features = features.reshape(UNITS, rows, sequences * SHARD)
    features, first = lax.optimization_barrier((features, first))
    x_parts = swap(features).reshape(HALF, sequences * SHARD)

    steps = RATIO // BATCH
    head_block = pl.BlockSpec((HALF, BATCH * HEAD), lambda h: (0, h))
    grad_block = pl.BlockSpec((HALF, BATCH * HEAD), lambda h: (0, steps + h))
    key_block = pl.BlockSpec((HALF, HEAD), lambda h: (0, 2 * RATIO))
    key_prev_block = pl.BlockSpec((HALF, HEAD), lambda h: (0, 2 * RATIO + 1))
    prev_block = pl.BlockSpec((HALF, HEAD), lambda h: (0, 0))
    p_block = pl.BlockSpec((BATCH, HALF, HALF), lambda h: (h, 0, 0))
    p_shape = pltpu.HBM((RATIO, HALF, HALF), BF16)

    product = 2 * RATIO * HALF * HALF * 3 // 2 * HEAD

    x_block = whole(tokens, width)
    prev_one = whole(HALF, HEAD)
    weights_own, weights_prev, dv_own, dv_prev = call(
        weights_kernel,
        2 * product,
        10 << 20,
        grid=(steps,),
        in_specs=[smem, head_block, key_block, key_prev_block, grad_block],
        out_specs=(p_block, p_block, prev_block, prev_block),
        out_shape=(p_shape, p_shape, pltpu.HBM((HALF, HEAD), F32), pltpu.HBM((HALF, HEAD), BF16)),
        scratch_shapes=[pltpu.VMEM((2 * HALF, HEAD), F32)],
        name="weights",
    )(flags, first, first, first, first)
    weights_own = pltpu.with_memory_space_constraint(weights_own, pltpu.HBM)
    weights_prev = pltpu.with_memory_space_constraint(weights_prev, pltpu.HBM)

    dv_next = lax.ppermute(dv_prev, both, to_before)
    parts_shape = pltpu.HBM((UNITS, rows, (1 + UNITS) * HEAD), BF16)
    parts = call(
        values_kernel,
        2 * tokens * width * KV * HEAD,
        4 << 20,
        grid=(sequences,),
        in_specs=[
            smem,
            pl.BlockSpec((HALF, SHARD), lambda i: (0, i)),
            whole(SHARD // 2, KV * HEAD),
            whole(SHARD // 2, KV * HEAD),
            whole(SHARD, RANK),
            whole(RANK, KV * HEAD),
        ],
        out_specs=pl.BlockSpec((KV, rows, (1 + UNITS) * HEAD), lambda i: (i, 0, 0)),
        out_shape=parts_shape,
        name="values",
    )(parity.astype(jnp.int32).reshape(1), x_parts, piece, piece_other, down_part, up_weight)
    merged = call(
        merge_kernel,
        0,
        1 << 19,
        grid=(1,),
        in_specs=[pl.BlockSpec(memory_space=pl.ANY), prev_one, prev_one],
        out_specs=whole(UNITS, rows, HEAD),
        out_shape=parts_shape,
        input_output_aliases={0: 0},
        name="merge",
    )(parts, dv_own, dv_next)
    third = swap(merged)
    v_unit = call(
        values_sum_kernel,
        1 << 20,
        1 << 20,
        grid=(1,),
        in_specs=[whole(UNITS, rows, (1 + UNITS) * HEAD)],
        out_specs=whole(HALF, HEAD),
        out_shape=pltpu.HBM((HALF, HEAD), BF16),
        name="values_sum",
    )(third)
    v_prev = lax.ppermute(v_unit, both, from_before)

    pieces = width // HEAD + KV
    peers = PLANES * weight_devices
    share = -(-pieces * RANK // peers)
    sums = call(
        adapter_kernel,
        4 * tokens * width * RANK,
        3 << 20,
        grid=(1,),
        in_specs=[
            whole(UNITS, rows, HEAD),
            x_block,
            whole(sequences, RANK, rows),
            whole(RANK, KV * HEAD),
        ],
        out_specs=whole(peers * share, HEAD),
        out_shape=pltpu.HBM((peers * share, HEAD), F32),
        name="adapter",
    )(third, x_rows, low_parts, up_weight)
    v_late, sums = lax.optimization_barrier((v_unit, sums))

    def among_peers(block):
        return lax.all_to_all(
            block, both, split_axis=0, concat_axis=0, axis_index_groups=same_unit, tiled=True
        ).reshape(peers, share, HEAD)

    mine = jnp.sum(among_peers(sums), axis=0) * (ADAPTER_SCALE / math.sqrt(tokens * devices))
    blank = jnp.zeros((rows // 2 - share, HEAD), BF16)
    high, rest = split_float(mine)
    mine_parts = jnp.concatenate([high, blank, rest, blank], axis=0)

    dq_unit, dk_own, dk_prev = call(
        score_grad_kernel,
        3 * product,
        12 << 20,
        grid=(steps,),
        in_specs=[
            smem,
            p_block,
            p_block,
            head_block,
            key_block,
            key_prev_block,
            grad_block,
            prev_block,
            prev_block,
        ],
        out_specs=(head_block, prev_block, prev_block),
        out_shape=(
            pltpu.HBM((HALF, wide), BF16),
            pltpu.HBM((HALF, HEAD), BF16),
            pltpu.HBM((HALF, HEAD), BF16),
        ),
        scratch_shapes=[pltpu.VMEM((2 * HALF, HEAD), F32), pltpu.VMEM((HEAD, 2 * HALF), BF16)],
        name="score_grad",
    )(
        flags,
        weights_own,
        weights_prev,
        first,
        first,
        first,
        first,
        v_late,
        v_prev,
    )
    returning = jnp.concatenate(
        [
            dq_unit.reshape(UNITS, rows, wide),
            dk_own.reshape(UNITS, rows, HEAD),
            dk_prev.reshape(UNITS, rows, HEAD),
            jnp.broadcast_to(mine_parts[None], (UNITS, rows, HEAD)),
        ],
        axis=2,
    )
    returned = swap(returning)

    sum_parts = returned[:, :, wide + 2 * HEAD :].reshape(UNITS * 2, rows // 2, HEAD)
    total = jnp.sum(sum_parts[:, :share].astype(F32), axis=0)
    spread = jnp.broadcast_to(total[None], (peers, share, HEAD)).reshape(peers * share, HEAD)
    key_prev = returned[:, :, wide + HEAD : wide + 2 * HEAD]
    key_prev, spread = lax.optimization_barrier((key_prev, spread))
    totals = among_peers(spread).reshape(peers * share, HEAD)[: pieces * RANK]
    totals = totals.reshape(pieces, RANK, HEAD)

    key_shape = jax.ShapeDtypeStruct((sequences, 1, rows, KV * HEAD), BF16)
    query_grad, key_own = call(
        unpack_kernel,
        0,
        4 << 20,
        grid=(sequences,),
        in_specs=[pl.BlockSpec((KV, rows, wide + HEAD), lambda i: (i, 0, 0))],
        out_specs=(token_wide, token_head),
        out_shape=(
            jax.ShapeDtypeStruct((sequences, 1, rows, KV * wide), BF16),
            jax.ShapeDtypeStruct((sequences, 1, rows, KV * HEAD), BF16),
        ),
        name="unpack",
    )(returned)
    key_next = lax.ppermute(key_prev, both, to_before)
    key_next = jnp.transpose(key_next.reshape(sequences, KV, rows, HEAD), (0, 2, 1, 3))
    key_next = key_next.reshape(sequences, 1, rows, KV * HEAD)
    key_grad = (key_own.astype(F32) + key_next.astype(F32)).astype(BF16)
    down_grad = jnp.transpose(totals[: width // HEAD], (0, 2, 1)).reshape(width, RANK)
    up_grad = jnp.transpose(totals[width // HEAD :], (1, 0, 2)).reshape(RANK, KV * HEAD)
    return (query_grad, key_grad, down_grad, up_grad)


def solution(mesh):
    tokens = P(None, "wt", "seq", None)
    return jax.shard_map(
        body,
        mesh=mesh,
        in_specs=(tokens, tokens, tokens, P("wt", None), P(), P(), tokens, P()),
        out_specs=(tokens, tokens, P(), P()),
        check_vma=False,
    )
```
